512 devices in a mesh: row: 16 (over x, y), col: 32 (over z, core).
Axes of the slice: x: 4, y: 4, z: 16, core: 2. Of those that a mesh axis runs over, the one named last changes fastest.
Arguments:
- covariates: bfloat16 [131072, 4096], P('row', 'col'), may hold values from -64 to 64
- labels: int32 [131072], P('row'), may hold values from 0 to 15
- weights: float32 [16, 4096], P(None, 'col'), may hold values from -0.0234375 to 0.0234375
- sample_index: int32 [65536], P('row'), may hold values from 0 to 131071, as said below
Outputs:
- gradient: float32 [16, 4096], P(None, 'col')
- newton_step: float32 [16, 4096], P(None, 'col')
The draws below stay inside these ranges and needn't reach their ends.
Inputs may be any that keep to these rules, and one draw needn't show every extreme that they name: The 4096 entries sample_index[b * 4096] to sample_index[(b + 1) * 4096 - 1] name users b * 8192 to (b + 1) * 8192 - 1; repeats may occur.
All inputs are finite; a program needn't handle non-finite values.
Results may differ from the reference program's by a relative error of at most 0.0039.
Values may be sent and summed in bfloat16 or wider, within the bound.
No kernel may reach another device: no remote copies, remote signals or barrier semaphores. Data moves between devices by JAX's collectives and lax.ppermute only.
A program may use at most 64 MiB of HBM per device.

```python
import jax
import jax.numpy as jnp
from jax import lax

P_SIZE = 4096
K = 16
ITERS = 2
U_DEV = 8192
SUB_DEV = 4096
USERS = 131072
SUB = 65536
N_ROW = 16
N_COL = 32


def draw_sample_index(key, part):
    key = jax.random.fold_in(key, 7)
    within = jax.random.randint(key, (SUB,), 0, U_DEV)
    position = jnp.arange(SUB)
    within = jnp.where(position == 0, 0, within)
    within = jnp.where(position == SUB - 1, U_DEV - 1, within)
    return (position // SUB_DEV * U_DEV + within).astype(jnp.int32)


def draw_covariates(key, part):
    key = jax.random.fold_in(key, 11)
    keys = jax.random.split(key, 6)
    block_cols = P_SIZE // N_COL
    spread = 1.0
    noise = jnp.clip(jax.random.normal(keys[5], (N_ROW, U_DEV, N_COL, block_cols), jnp.float32), -4.0, 4.0)
    levels = jnp.exp(jax.random.uniform(keys[0], (N_ROW, N_COL), jnp.float32, -spread, spread))
    chance = jax.random.uniform(keys[1], (N_ROW, U_DEV), jnp.float32)
    forced = jax.random.randint(keys[2], (N_ROW, 1), 0, U_DEV)
    position = jnp.arange(U_DEV)[None, :]
    heavy = jnp.logical_or(chance < 1.0 / 256.0, position == forced)
    heavy_scale = jnp.exp(jax.random.uniform(keys[3], (N_ROW, U_DEV), jnp.float32, 1.386, 2.079))
    light_scale = jnp.exp(jax.random.uniform(keys[4], (N_ROW, U_DEV), jnp.float32, -2.303, -1.05))
    scale = jnp.where(heavy, heavy_scale, light_scale)
    values = noise * levels[:, None, :, None] * scale[:, :, None, None]
    values = jnp.clip(values, -64.0, 64.0)
    return values.reshape(USERS, P_SIZE).astype(jnp.bfloat16)


def place_ends(drawn, own_key, least, largest):
    spot = [jax.random.randint(jax.random.fold_in(own_key, axis), (), 0, length) for axis, length in enumerate(drawn.shape)]
    widest = drawn.shape.index(max(drawn.shape))
    next_to = spot[:widest] + [(spot[widest] + 1) % drawn.shape[widest]] + spot[widest + 1:]
    return drawn.at[tuple(spot)].set(least).at[tuple(next_to)].set(largest)


def level_of(key, shape, cuts, least, top_value):
    gain, own = 1.0, jax.random.fold_in(key, 6)
    for dim, blocks in cuts:
        steps = jnp.exp(jax.random.uniform(jax.random.fold_in(own, dim), (blocks,), jnp.float32, least / len(cuts), top_value / len(cuts)))
        gain = gain * jnp.repeat(steps, shape[dim] // blocks).reshape([-1 if axis == dim else 1 for axis in range(len(shape))])
    return gain


def gaussian(rng, extent, scale, reach, cuts=(), dtype=jnp.bfloat16):
    gain = level_of(rng, extent, cuts, -0.22, 0.18) if cuts else 1.0
    values = jax.random.normal(rng, extent, jnp.float32) * scale * gain
    return jnp.minimum(jnp.maximum(values, -reach), reach).astype(dtype)


def setup_inputs(seed: int = 0) -> dict:
    seeds = jax.random.split(jax.random.key(seed), 5)
    covariates = draw_covariates(jax.random.fold_in(seeds[4], 71), 0)
    labels = place_ends(jax.random.randint(seeds[1], (USERS,), 0, K), jax.random.fold_in(seeds[1], 1), 0, K - 1).astype(jnp.int32)
    weights = gaussian(seeds[2], (K, P_SIZE), (16 * P_SIZE) ** -0.5, 0.0234375, ((1, 32),), jnp.float32)
    sample_index = draw_sample_index(jax.random.fold_in(seeds[4], 71), 0)
    return dict(covariates=covariates, labels=labels, weights=weights, sample_index=sample_index)


RIDGE_WEIGHT = 0.004


def class_shares(logits):
    exponent = jnp.exp(logits)
    return exponent / jnp.sum(exponent, axis=0, keepdims=True)


def reference(covariates, labels, weights, sample_index):
    rounded_weights = weights.astype(jnp.bfloat16)
    logits = lax.dot_general(rounded_weights, covariates, (((1,), (1,)), ((), ())), preferred_element_type=jnp.float32)
    shares = class_shares(logits)
    classes = lax.broadcasted_iota(jnp.int32, shares.shape, 0)
    indicator = (labels[None, :] == classes).astype(jnp.float32)
    misfit = (shares - indicator).astype(jnp.bfloat16)
    gradient = jnp.dot(misfit, covariates, preferred_element_type=jnp.float32) / USERS + RIDGE_WEIGHT * weights
    sub_rows = jnp.take(covariates, sample_index.astype(jnp.int32), axis=0)
    sub_shares = jnp.take(shares, sample_index.astype(jnp.int32), axis=1)

    def hessian_apply(vector):
        rounded = vector.astype(jnp.bfloat16)
        response = lax.dot_general(rounded, sub_rows, (((1,), (1,)), ((), ())), preferred_element_type=jnp.float32)
        centred = response - jnp.sum(sub_shares * response, axis=0, keepdims=True)
        weighted = (sub_shares * centred).astype(jnp.bfloat16)
        return jnp.dot(weighted, sub_rows, preferred_element_type=jnp.float32) / SUB + RIDGE_WEIGHT * vector

    newton_step = jnp.zeros_like(weights)
    residual = -gradient
    direction = residual
    norm_now = jnp.sum(residual * residual)
    for iteration in range(ITERS):
        image = hessian_apply(direction)
        step_size = norm_now / jnp.sum(direction * image)
        newton_step = newton_step + step_size * direction
        residual = residual - step_size * image
        if iteration + 1 < ITERS:
            norm_new = jnp.sum(residual * residual)
            direction = residual + (norm_new / norm_now) * direction
            norm_now = norm_new
    return gradient, newton_step
```

```python
import jax
import jax.numpy as jnp
from jax import lax
from jax.sharding import Mesh, PartitionSpec as P

RIDGE_WEIGHT = 0.004


def class_shares(logits):
    exponent = jnp.exp(logits)
    return exponent / jnp.sum(exponent, axis=0, keepdims=True)


def swap(block, axis):
    return lax.all_to_all(block, axis, 0, 0, tiled=True)


def spread(block, axis):
    return swap(jnp.broadcast_to(block[None], (lax.axis_size(axis),) + block.shape), axis)


def total(block, axis):
    return jnp.sum(spread(block, axis), axis=0)


def body(covariates, labels, weights, sample_index):
    user_rows, col_width = covariates.shape
    row_count, depth, cores = lax.axis_size("row"), lax.axis_size("z"), lax.axis_size("c")
    row, level, core = lax.axis_index("row"), lax.axis_index("z"), lax.axis_index("c")
    users = user_rows * row_count
    sub_total = sample_index.shape[0] * row_count
    half = user_rows // cores
    own = half // depth
    first_own = core * half + level * own
    classes = weights.shape[0]

    other = lax.dynamic_slice_in_dim(covariates, (1 - core) * half, half, 0)
    other = lax.ppermute(other, "c", [(0, 1), (1, 0)])
    mine = lax.dynamic_slice_in_dim(covariates, core * half, half, 0)
    wide = jnp.where(core == 0, jnp.concatenate([mine, other], 1), jnp.concatenate([other, mine], 1))
    wide_weights = lax.all_gather(weights, "c", axis=1, tiled=True)

    position = row * user_rows + first_own + jnp.arange(own, dtype=jnp.int32)
    count = jnp.sum((sample_index[:, None] == position[None, :]).astype(jnp.float32), axis=0)

    def pieces(values):
        return values.reshape(classes, depth, own).transpose(1, 0, 2)

    def reduce_users(values):
        return jnp.sum(swap(pieces(values).astype(jnp.bfloat16), "z").astype(jnp.float32), axis=0)

    def back_to_columns(block):
        gathered = spread(block.astype(jnp.bfloat16), "z").transpose(1, 0, 2).reshape(classes, half)
        part = jnp.dot(gathered, wide, preferred_element_type=jnp.float32)
        part = jnp.sum(lax.all_gather(part, "c", axis=0), axis=0)
        return total(part, "row")

    def respond(vector):
        return lax.dot_general(
            vector.astype(jnp.bfloat16), wide, (((1,), (1,)), ((), ())), preferred_element_type=jnp.float32
        )

    partial_value = lax.dot_general(
        weights.astype(jnp.bfloat16), covariates, (((1,), (1,)), ((), ())), preferred_element_type=jnp.float32
    )
    both = lax.all_gather(partial_value.astype(jnp.bfloat16), "c", axis=0)
    both = lax.dynamic_slice_in_dim(both, core * half, half, 2).astype(jnp.float32)
    logits = reduce_users(jnp.sum(both, axis=0))
    shares = class_shares(logits)
    own_labels = lax.dynamic_slice_in_dim(labels, first_own, own, 0)
    indicator = own_labels[None, :] == lax.broadcasted_iota(jnp.int32, shares.shape, 0)
    misfit = shares - indicator.astype(jnp.float32)
    gradient = back_to_columns(misfit) / users + RIDGE_WEIGHT * wide_weights

    residual = -gradient
    response = reduce_users(respond(residual))
    centred = response - jnp.sum(shares * response, axis=0, keepdims=True)
    image = back_to_columns(count * shares * centred) / sub_total + RIDGE_WEIGHT * residual

    scalars = jnp.stack([jnp.sum(residual * residual), jnp.sum(residual * image), jnp.sum(image * image)])
    scalars = total(jnp.pad(scalars, (0, 125))[None], "z")[0]
    image_response = reduce_users(respond(image))
    norm_0, curve_0, image_norm = scalars[0], scalars[1], scalars[2]
    step_0 = norm_0 / curve_0
    beta = jnp.maximum(image_norm / curve_0 * step_0 - 1.0, 0.0)
    residual_1 = residual - step_0 * image
    direction_1 = residual_1 + beta * residual
    response_1 = (1.0 + beta) * response - step_0 * image_response
    centred_1 = response_1 - jnp.sum(shares * response_1, axis=0, keepdims=True)
    spread_1 = jnp.sum(count * shares * centred_1 * centred_1)
    last = jnp.stack([jnp.sum(residual_1 * residual_1), jnp.sum(direction_1 * direction_1), spread_1])
    last = total(jnp.pad(last, (0, 125))[None], "z")
    last = total(last, ("row", "c"))[0]
    copies = row_count * cores
    norm_1, square_1 = last[0] / copies, last[1] / copies
    curve_1 = last[2] / sub_total + RIDGE_WEIGHT * square_1
    newton_step = step_0 * residual + norm_1 / curve_1 * direction_1

    def own_columns(block):
        return lax.dynamic_slice_in_dim(block, core * col_width, col_width, 1)

    return (own_columns(gradient), own_columns(newton_step))


def solution(mesh):
    cores = 2
    rows, cols = mesh.devices.shape
    fine = Mesh(mesh.devices.reshape(rows, cols // cores, cores), ("row", "z", "c"))
    in_specs = (P("row", ("z", "c")), P("row"), P(None, ("z", "c")), P("row"))
    out_specs = (P(None, ("z", "c")), P(None, ("z", "c")))
    return jax.shard_map(body, mesh=fine, in_specs=in_specs, out_specs=out_specs, check_vma=False)
```

```python
import functools

import jax
import jax.numpy as jnp
from jax import lax
from jax.experimental import pallas as pl
from jax.experimental.pallas import tpu as pltpu
from jax.sharding import Mesh, PartitionSpec as P

RIDGE_WEIGHT = 0.004
F32, BF16 = jnp.float32, jnp.bfloat16
LANES = 128
PIECES = 3
CORES = 2


def kernel_call(body, out_shape, *operands):
    return pl.pallas_call(
        body,
        out_shape=out_shape,
        in_specs=[pl.BlockSpec(memory_space=pltpu.VMEM)] * len(operands),
        out_specs=jax.tree.map(lambda _: pl.BlockSpec(memory_space=pltpu.VMEM), out_shape),
        compiler_params=pltpu.CompilerParams(vmem_limit_bytes=24 * 1024 * 1024),
    )(*operands)


def times_transposed(left, right):
    return lax.dot_general(left, right, (((1,), (1,)), ((), ())), preferred_element_type=F32)


def arrived(ref):
    total = ref[0].astype(F32)
    for sender in range(1, ref.shape[0]):
        total = total + ref[sender].astype(F32)
    return total


def repeat(ref, block):
    for receiver in range(ref.shape[0]):
        ref[receiver] = block


def shares_sum(shares, block):
    return jnp.sum(shares * block, axis=0, keepdims=True)


def whole(block):
    return jnp.sum(jnp.sum(block, axis=1, keepdims=True), axis=0, keepdims=True)


def logits_kernel(weights, rows, mine, other):
    core = lax.axis_index("c")
    depth = mine.shape[0]
    rounded = weights[...].astype(BF16)
    for level in range(depth):
        mine[level] = times_transposed(rounded, rows[core * depth + level])
        other[level] = times_transposed(rounded, rows[(1 - core) * depth + level])


def add_kernel(mine, other, both):
    both[...] = mine[...] + other[...]


def misfit_kernel(came, labels, shares, sent):
    depth = came.shape[0]
    place = lax.axis_index("c") * depth + lax.axis_index("z")
    exponent = jnp.exp(arrived(came))
    share = exponent / jnp.sum(exponent, axis=0, keepdims=True)
    shares[...] = share
    indicator = labels[pl.ds(place, 1), :] == lax.broadcasted_iota(jnp.int32, share.shape, 0)
    repeat(sent, (share - indicator.astype(F32)).astype(BF16))


def columns_kernel(came, rows, others, part):
    core = lax.axis_index("c")
    depth, width = came.shape[0], rows.shape[2]
    own = jnp.zeros((part.shape[0], width), F32)
    far = jnp.zeros((part.shape[0], width), F32)
    for level in range(depth):
        own = own + jnp.dot(came[level], rows[core * depth + level], preferred_element_type=F32)
        far = far + jnp.dot(came[level], others[level], preferred_element_type=F32)
    part[:, :width] = own
    part[:, width:] = far


def pair_kernel(parts, sent):
    core = lax.axis_index("c")
    mine, far = parts[core], parts[1 - core]
    width = mine.shape[1] // CORES
    repeat(sent, mine + jnp.concatenate([far[:, width:], far[:, :width]], axis=1))


def respond(vector, rows, others, sent):
    core = lax.axis_index("c")
    depth, width = others.shape[0], rows.shape[2]
    own, far = vector[:, :width].astype(BF16), vector[:, width:].astype(BF16)
    for level in range(depth):
        value = times_transposed(own, rows[core * depth + level]) + times_transposed(far, others[level])
        sent[level, :, : value.shape[1]] = value.astype(BF16)


def gradient_kernel(users, came, weights, far_weights, rows, others, gradient, residual, sent):
    width = weights.shape[1]
    value = arrived(came) / users + RIDGE_WEIGHT * jnp.concatenate([weights[...], far_weights[...]], axis=1)
    gradient[...] = value[:, :width]
    residual[...] = -value
    respond(-value, rows, others, sent)


def weigh_kernel(came, shares, count, response, sent):
    value = arrived(came)
    response[...] = value
    share = shares[...]
    repeat(sent, (count[...] * (share * (value - shares_sum(share, value)))).astype(BF16))


def image_kernel(sub_total, came, residual, rows, others, image, sent):
    start = residual[...]
    value = arrived(came) / sub_total + RIDGE_WEIGHT * start
    image[...] = value
    respond(value, rows, others, sent)
    place = lax.broadcasted_iota(jnp.int32, (start.shape[0], LANES), 0)
    tile = jnp.zeros(place.shape, F32)
    for which, product in enumerate((start * start, start * value, value * value)):
        left = whole(product)
        for piece in range(PIECES):
            head = left.astype(BF16).astype(F32)
            tile = jnp.where(place == which * PIECES + piece, head, tile)
            left = left - head
    tile = tile.astype(BF16)
    for level in range(sent.shape[0]):
        sent[level, :, value.shape[1] :] = tile


def direction_kernel(came, response, shares, count, residual, image, base, direction, sent):
    got = arrived(came)
    width = base.shape[1]
    image_response, tile = got[:, : count.shape[1]], got[:, count.shape[1] :]

    def scalar(which):
        return sum(tile[which * PIECES + piece : which * PIECES + piece + 1, :1] for piece in range(PIECES))

    norm, curve, image_norm = scalar(0), scalar(1), scalar(2)
    step = norm / curve
    beta = jnp.maximum(image_norm / curve * step - 1.0, 0.0)
    start = residual[...]
    after = start - step * image[...]
    second = after + beta * start
    base[...] = step * start[:, :width]
    direction[...] = second[:, :width]
    share = shares[...]
    value = (1.0 + beta) * response[...] - step * image_response
    centred = value - shares_sum(share, value)
    lane = lax.broadcasted_iota(jnp.int32, (1, LANES), 1)
    line = jnp.where(lane == 0, whole(after * after), whole(second * second))
    line = jnp.where(lane < 2, line, whole(count[...] * (share * (centred * centred))))
    repeat(sent, line)


def relay_kernel(came, sent):
    repeat(sent, arrived(came))


def step_kernel(sub_total, copies, came, base, direction, newton_step):
    line = arrived(came)
    norm, square, spread = line[:, 0:1] / copies, line[:, 1:2] / copies, line[:, 2:3]
    curve = spread / sub_total + RIDGE_WEIGHT * square
    newton_step[...] = base[...] + norm / curve * direction[...]


def swap(block, axis):
    return lax.all_to_all(block, axis, 0, 0, tiled=True)


def array(*shape, dtype=F32):
    return jax.ShapeDtypeStruct(shape, dtype)


def body(covariates, labels, weights, sample_index):
    user_rows, width = covariates.shape
    classes = weights.shape[0]
    row_count, depth = lax.axis_size("row"), lax.axis_size("z")
    row, level, core = lax.axis_index("row"), lax.axis_index("z"), lax.axis_index("c")
    users = user_rows * row_count
    sub_total = sample_index.shape[0] * row_count
    half = user_rows // CORES
    own = half // depth
    wide = CORES * width
    pair = [(0, 1), (1, 0)]
    rows = covariates.reshape(CORES * depth, own, width)
    labels = labels.reshape(CORES * depth, own)
    blocks = (depth, classes, own)

    mine, other = kernel_call(logits_kernel, (array(*blocks), array(*blocks)), weights, rows)
    logits = kernel_call(add_kernel, array(*blocks), mine, lax.ppermute(other, "c", pair))
    logits, covariates, weights, sample_index = lax.optimization_barrier(
        (logits, covariates, weights, sample_index)
    )
    came = swap(logits, "z")
    others = lax.dynamic_slice_in_dim(covariates, (1 - core) * half, half, 0)
    others = lax.ppermute(others, "c", pair).reshape(depth, own, width)
    far_weights = lax.ppermute(weights, "c", pair)
    position = row * user_rows + core * half + level * own + jnp.arange(own, dtype=jnp.int32)
    count = jnp.sum((sample_index[:, None] == position[None, :]).astype(F32), axis=0)[None]
    came, others, far_weights, count = lax.optimization_barrier((came, others, far_weights, count))

    shares, sent = kernel_call(misfit_kernel, (array(classes, own), array(*blocks, dtype=BF16)), came, labels)

    def back_to_columns(sent):
        part = kernel_call(columns_kernel, array(classes, wide), swap(sent, "z"), rows, others)
        parts = lax.all_gather(part, "c", axis=0)
        return swap(kernel_call(pair_kernel, array(row_count, classes, wide), parts), "row")

    gradient, residual, sent = kernel_call(
        functools.partial(gradient_kernel, users),
        (array(classes, width), array(classes, wide), array(*blocks, dtype=BF16)),
        back_to_columns(sent), weights, far_weights, rows, others,
    )
    response, sent = kernel_call(
        weigh_kernel, (array(classes, own), array(*blocks, dtype=BF16)), swap(sent, "z"), shares, count
    )
    image, sent = kernel_call(
        functools.partial(image_kernel, sub_total),
        (array(classes, wide), array(depth, classes, own + LANES, dtype=BF16)),
        back_to_columns(sent), residual, rows, others,
    )
    base, direction, sent = kernel_call(
        direction_kernel,
        (array(classes, width), array(classes, width), array(depth, 1, LANES)),
        swap(sent, "z"), response, shares, count, residual, image,
    )
    sent = kernel_call(relay_kernel, array(row_count * CORES, 1, LANES), swap(sent, "z"))
    newton_step = kernel_call(
        functools.partial(step_kernel, sub_total, row_count * CORES),
        array(classes, width),
        swap(sent, ("row", "c")), base, direction,
    )
    return gradient, newton_step


def solution(mesh):
    rows, cols = mesh.devices.shape
    fine = Mesh(mesh.devices.reshape(rows, cols // CORES, CORES), ("row", "z", "c"))
    in_specs = (P("row", ("z", "c")), P("row"), P(None, ("z", "c")), P("row"))
    out_specs = (P(None, ("z", "c")), P(None, ("z", "c")))
    return jax.shard_map(body, mesh=fine, in_specs=in_specs, out_specs=out_specs, check_vma=False)
```

```python
import functools

import jax
import jax.numpy as jnp
from jax import lax
from jax.experimental import pallas as pl
from jax.experimental.pallas import tpu as pltpu
from jax.sharding import Mesh, PartitionSpec as P

RIDGE_WEIGHT = 0.004
F32, BF16 = jnp.float32, jnp.bfloat16
LANES, SUBLANES = 128, 8
PIECES = 3
CORES = 2
GROUPS = 4
TOP, REACH = 32767.0, 768.0


def kernel_call(body, out_shape, *operands):
    return pl.pallas_call(
        body,
        out_shape=out_shape,
        in_specs=[pl.BlockSpec(memory_space=pltpu.VMEM)] * len(operands),
        out_specs=jax.tree.map(lambda _: pl.BlockSpec(memory_space=pltpu.VMEM), out_shape),
        compiler_params=pltpu.CompilerParams(vmem_limit_bytes=24 * 1024 * 1024),
    )(*operands)


def times_transposed(left, right):
    return lax.dot_general(left, right, (((1,), (1,)), ((), ())), preferred_element_type=F32)


def arrived(ref):
    total = ref[0].astype(F32)
    for sender in range(1, ref.shape[0]):
        total = total + ref[sender].astype(F32)
    return total


def repeat(ref, block):
    for receiver in range(ref.shape[0]):
        ref[receiver] = block


def shares_sum(shares, block):
    return jnp.sum(shares * block, axis=0, keepdims=True)


def whole(block):
    return jnp.sum(jnp.sum(block, axis=1, keepdims=True), axis=0, keepdims=True)


def send_other_kernel(weights_hbm, rows_hbm, other, weights, rows, weights_sem, row_sems):
    depth = other.shape[0]
    first = (1 - lax.axis_index("c")) * depth
    head = pltpu.make_async_copy(weights_hbm, weights, weights_sem)
    head.start()
    step = depth // GROUPS
    copies = []
    for group in range(GROUPS):
        here = pl.ds(group * step, step)
        copies.append(
            pltpu.make_async_copy(rows_hbm.at[pl.ds(first + group * step, step)], rows.at[here], row_sems.at[group])
        )
        copies[-1].start()
    head.wait()
    rounded = weights[...].astype(BF16)
    for group in range(GROUPS):
        copies[group].wait()
        for level in range(group * step, (group + 1) * step):
            other[level] = times_transposed(rounded, rows[level])


def keep_kernel(user_rows, weights, rows, index, mine, count):
    depth, _, own = mine.shape
    core = lax.axis_index("c")
    place = core * depth + lax.axis_index("z")
    rounded = weights[...].astype(BF16)
    for level in range(depth):
        mine[level] = times_transposed(rounded, rows[core * depth + level])
    offset = index[...] - (lax.axis_index("row") * user_rows + place * own)
    low, high = offset & (LANES - 1), offset >> 7
    low_place = lax.broadcasted_iota(jnp.int32, (LANES, LANES), 0)
    high_place = lax.broadcasted_iota(jnp.int32, (SUBLANES, LANES), 0)
    drawn = jnp.zeros((SUBLANES, LANES), F32)
    for line in range(index.shape[0]):
        is_low = (low[line : line + 1] == low_place).astype(F32).astype(BF16)
        is_high = (high[line : line + 1] == high_place).astype(F32).astype(BF16)
        drawn = drawn + times_transposed(is_high, is_low)
    for part in range(own // LANES):
        count[:, part * LANES : (part + 1) * LANES] = drawn[part : part + 1]


def code_kernel(mine, other, sent):
    for level in range(mine.shape[0]):
        value = mine[level] + other[level]
        value = value - value[-1:]
        largest = jnp.max(jnp.abs(value), axis=0, keepdims=True)
        scale = jnp.minimum(jnp.floor(largest * (TOP / REACH)) + 1.0, TOP)
        code = jnp.floor(value * (TOP * TOP / REACH / scale) + 0.5)
        code = jnp.clip(code, -TOP, TOP)
        last = lax.broadcasted_iota(jnp.int32, value.shape, 0) == value.shape[0] - 1
        sent[level] = jnp.where(last, scale, code).astype(jnp.int32).astype(jnp.int16)


def misfit_kernel(came, labels, shares, sent):
    depth, classes, own = came.shape
    logits = jnp.zeros((classes, own), F32)
    for sender in range(depth):
        code = came[sender].astype(jnp.int32).astype(F32)
        logits = logits + code * (code[-1:] * (REACH / TOP / TOP))
    kind = lax.broadcasted_iota(jnp.int32, logits.shape, 0)
    logits = jnp.where(kind == classes - 1, 0.0, logits)
    exponent = jnp.exp(logits - jnp.max(logits, axis=0, keepdims=True))
    share = exponent / jnp.sum(exponent, axis=0, keepdims=True)
    shares[...] = share
    lines = own // LANES
    first = (lax.axis_index("c") * depth + lax.axis_index("z")) * lines
    label = jnp.concatenate([labels[pl.ds(first + line, 1), :] for line in range(lines)], axis=1)
    repeat(sent, (share - (label == kind).astype(F32)).astype(BF16))


def columns(came, rows):
    core = lax.axis_index("c")
    depth = came.shape[0]
    sums = []
    for owner in (core, 1 - core):
        first = (owner * CORES + core) * depth
        total = jnp.dot(came[0], rows[first], preferred_element_type=F32)
        for level in range(1, depth):
            total = total + jnp.dot(came[level], rows[first + level], preferred_element_type=F32)
        sums.append(total)
    return sums


def misfit_columns_kernel(ridge, came, rows, weights, part):
    own, far = columns(came, rows)
    width = own.shape[1]
    part[:, :width] = own + ridge * weights[...]
    part[:, width:] = far


def image_columns_kernel(came, rows, part):
    own, far = columns(came, rows)
    width = own.shape[1]
    part[:, :width] = own
    part[:, width:] = far


def pair_kernel(parts, sent):
    core = lax.axis_index("c")
    mine, far = parts[core], parts[1 - core]
    width = mine.shape[1] // CORES
    both = mine + jnp.concatenate([far[:, width:], far[:, :width]], axis=1)
    repeat(sent, both.astype(sent.dtype))


def respond(vector, rows, depth):
    core = lax.axis_index("c")
    width = rows.shape[2]
    own, far = vector[:, :width].astype(BF16), vector[:, width:].astype(BF16)
    for level in range(depth):
        near = times_transposed(own, rows[(core * CORES + core) * depth + level])
        yield near + times_transposed(far, rows[((1 - core) * CORES + core) * depth + level])


def gradient_kernel(users, came, rows, gradient, residual, sent):
    width = gradient.shape[1]
    value = arrived(came) / users
    gradient[...] = value[:, :width]
    residual[...] = -value
    for level, answer in enumerate(respond(-value, rows, sent.shape[0])):
        sent[level] = answer.astype(BF16)


def weigh_kernel(came, shares, count, response, sent):
    value = arrived(came)
    response[...] = value
    share = shares[...]
    repeat(sent, (count[...] * (share * (value - shares_sum(share, value)))).astype(BF16))


def image_kernel(sub_total, came, residual, rows, image, sent):
    start = residual[...]
    value = arrived(came) / sub_total + RIDGE_WEIGHT * start
    image[...] = value
    _, classes, own = sent.shape
    lane = lax.broadcasted_iota(jnp.int32, (1, own), 1)
    line = jnp.zeros(lane.shape, F32)
    for which, product in enumerate((start * start, start * value, value * value)):
        left = whole(product)
        for piece in range(PIECES):
            head = left.astype(BF16).astype(F32)
            line = jnp.where(lane == which * PIECES + piece, head, line)
            left = left - head
    last = lax.broadcasted_iota(jnp.int32, (classes, own), 0) == classes - 1
    for level, answer in enumerate(respond(value, rows, sent.shape[0])):
        sent[level] = jnp.where(last, line, answer - answer[-1:]).astype(BF16)


def direction_kernel(came, response, shares, count, residual, image, base, direction, sent):
    got = arrived(came)
    classes, own = got.shape
    width = base.shape[1]
    line = got[-1:]
    lane = lax.broadcasted_iota(jnp.int32, line.shape, 1)

    def scalar(which):
        pieces = jnp.logical_and(lane >= which * PIECES, lane < (which + 1) * PIECES)
        return jnp.sum(jnp.where(pieces, line, 0.0), axis=1, keepdims=True)

    norm, curve, image_norm = scalar(0), scalar(1), scalar(2)
    step = norm / curve
    beta = jnp.maximum(image_norm / curve * step - 1.0, 0.0)
    start = residual[...]
    after = start - step * image[...]
    second = after + beta * start
    base[...] = step * start[:, :width]
    direction[...] = second[:, :width]
    image_response = jnp.where(lax.broadcasted_iota(jnp.int32, got.shape, 0) == classes - 1, 0.0, got)
    share = shares[...]
    value = (1.0 + beta) * response[...] - step * image_response
    centred = value - shares_sum(share, value)
    lane = lax.broadcasted_iota(jnp.int32, (1, LANES), 1)
    line = jnp.where(lane == 0, whole(after * after), whole(second * second))
    line = jnp.where(lane < 2, line, whole(count[...] * (share * (centred * centred))))
    repeat(sent, line)


def relay_kernel(came, sent):
    repeat(sent, arrived(came))


def step_kernel(sub_total, copies, came, base, direction, newton_step):
    line = arrived(came)
    norm, square, spread = line[:, 0:1] / copies, line[:, 1:2] / copies, line[:, 2:3]
    curve = spread / sub_total + RIDGE_WEIGHT * square
    newton_step[...] = base[...] + norm / curve * direction[...]


def swap(block, axis):
    return lax.all_to_all(block, axis, 0, 0, tiled=True)


def array(*shape, dtype=F32):
    return jax.ShapeDtypeStruct(shape, dtype)


def body(covariates, labels, weights, sample_index):
    user_rows, width = covariates.shape
    classes = weights.shape[0]
    row_count, depth = lax.axis_size("row"), lax.axis_size("z")
    users = user_rows * row_count
    sub_total = sample_index.shape[0] * row_count
    own = user_rows // CORES // depth
    wide = CORES * width
    blocks = (depth, classes, own)
    rows = covariates.reshape(CORES * depth, own, width)
    labels = labels.reshape(-1, LANES)
    sample_index = sample_index.reshape(-1, LANES)

    pair_rows = lax.all_gather(rows, "c", axis=0, tiled=True)
    other = pl.pallas_call(
        send_other_kernel,
        out_shape=array(*blocks),
        in_specs=[pl.BlockSpec(memory_space=pl.ANY)] * 2,
        out_specs=pl.BlockSpec(memory_space=pltpu.VMEM),
        scratch_shapes=[
            pltpu.VMEM(weights.shape, F32),
            pltpu.VMEM((depth, own, width), BF16),
            pltpu.SemaphoreType.DMA,
            pltpu.SemaphoreType.DMA((GROUPS,)),
        ],
    )(weights, rows)
    other = lax.ppermute(other, "c", [(0, 1), (1, 0)])
    mine, count = kernel_call(
        functools.partial(keep_kernel, user_rows), (array(*blocks), array(1, own)), weights, rows, sample_index
    )
    sent = kernel_call(code_kernel, array(*blocks, dtype=jnp.int16), mine, other)
    shares, sent = kernel_call(
        misfit_kernel, (array(classes, own), array(*blocks, dtype=BF16)), swap(sent, "z"), labels
    )

    def add_pair(part, dtype):
        parts = lax.all_gather(part, "c", axis=0)
        return swap(kernel_call(pair_kernel, array(row_count, classes, wide, dtype=dtype), parts), "row")

    ridge = RIDGE_WEIGHT * users / row_count
    part = kernel_call(
        functools.partial(misfit_columns_kernel, ridge), array(classes, wide), swap(sent, "z"), pair_rows, weights
    )
    gradient, residual, sent = kernel_call(
        functools.partial(gradient_kernel, users),
        (array(classes, width), array(classes, wide), array(*blocks, dtype=BF16)),
        add_pair(part, F32), pair_rows,
    )
    response, sent = kernel_call(
        weigh_kernel, (array(classes, own), array(*blocks, dtype=BF16)), swap(sent, "z"), shares, count
    )
    part = kernel_call(image_columns_kernel, array(classes, wide), swap(sent, "z"), pair_rows)
    image, sent = kernel_call(
        functools.partial(image_kernel, sub_total),
        (array(classes, wide), array(*blocks, dtype=BF16)),
        add_pair(part, BF16), residual, pair_rows,
    )
    base, direction, sent = kernel_call(
        direction_kernel,
        (array(classes, width), array(classes, width), array(depth, 1, LANES)),
        swap(sent, "z"), response, shares, count, residual, image,
    )
    sent = kernel_call(relay_kernel, array(row_count * CORES, 1, LANES), swap(sent, "z"))
    newton_step = kernel_call(
        functools.partial(step_kernel, sub_total, row_count * CORES),
        array(classes, width),
        swap(sent, ("row", "c")), base, direction,
    )
    return gradient, newton_step


def solution(mesh):
    rows, cols = mesh.devices.shape
    fine = Mesh(mesh.devices.reshape(rows, cols // CORES, CORES), ("row", "z", "c"))
    in_specs = (P("row", ("z", "c")), P("row"), P(None, ("z", "c")), P("row"))
    out_specs = (P(None, ("z", "c")), P(None, ("z", "c")))
    return jax.shard_map(body, mesh=fine, in_specs=in_specs, out_specs=out_specs, check_vma=False)
```

```python
import functools

import jax
import jax.numpy as jnp
from jax import lax
from jax.experimental import pallas as pl
from jax.experimental.pallas import tpu as pltpu
from jax.sharding import Mesh, PartitionSpec as P

RIDGE_WEIGHT = 0.004
F32, BF16 = jnp.float32, jnp.bfloat16
LANES, SUBLANES = 128, 8
PIECES = 3
CORES = 2
TOP, REACH = 32767.0, 768.0


def kernel_call(body, out_shape, *operands):
    return pl.pallas_call(
        body,
        out_shape=out_shape,
        in_specs=[pl.BlockSpec(memory_space=pltpu.VMEM)] * len(operands),
        out_specs=jax.tree.map(lambda _: pl.BlockSpec(memory_space=pltpu.VMEM), out_shape),
        compiler_params=pltpu.CompilerParams(vmem_limit_bytes=24 * 1024 * 1024),
    )(*operands)


def times_transposed(left, right):
    return lax.dot_general(left, right, (((1,), (1,)), ((), ())), preferred_element_type=F32)


def arrived(ref):
    total = ref[0].astype(F32)
    for sender in range(1, ref.shape[0]):
        total = total + ref[sender].astype(F32)
    return total


def repeat(ref, block):
    for receiver in range(ref.shape[0]):
        ref[receiver] = block


def shares_sum(shares, block):
    return jnp.sum(shares * block, axis=0, keepdims=True)


def whole(block):
    return jnp.sum(jnp.sum(block, axis=1, keepdims=True), axis=0, keepdims=True)


def count_kernel(user_rows, depth, index, count):
    own = count.shape[1]
    place = lax.axis_index("c") * depth + lax.axis_index("z")
    offset = index[...] - (lax.axis_index("row") * user_rows + place * own)
    low, high = offset & (LANES - 1), offset >> 7
    low_place = lax.broadcasted_iota(jnp.int32, (LANES, LANES), 0)
    high_place = lax.broadcasted_iota(jnp.int32, (SUBLANES, LANES), 0)
    drawn = jnp.zeros((SUBLANES, LANES), F32)
    for line in range(index.shape[0]):
        is_low = (low[line : line + 1] == low_place).astype(F32).astype(BF16)
        is_high = (high[line : line + 1] == high_place).astype(F32).astype(BF16)
        drawn = drawn + times_transposed(is_high, is_low)
    for part in range(own // LANES):
        count[:, part * LANES : (part + 1) * LANES] = drawn[part : part + 1]


def code_kernel(pair_weights, rows, sent):
    depth = sent.shape[0]
    rounded = [pair_weights[core].astype(BF16) for core in range(CORES)]
    for level in range(depth):
        value = sum(times_transposed(rounded[core], rows[core * depth + level]) for core in range(CORES))
        value = value - value[-1:]
        largest = jnp.max(jnp.abs(value), axis=0, keepdims=True)
        scale = jnp.minimum(jnp.floor(largest * (TOP / REACH)) + 1.0, TOP)
        code = jnp.floor(value * (TOP * TOP / REACH / scale) + 0.5)
        code = jnp.clip(code, -TOP, TOP)
        last = lax.broadcasted_iota(jnp.int32, value.shape, 0) == value.shape[0] - 1
        sent[level] = jnp.where(last, scale, code).astype(jnp.int32).astype(jnp.int16)


def misfit_kernel(came, labels, shares, sent):
    depth, classes, own = came.shape
    logits = jnp.zeros((classes, own), F32)
    for sender in range(depth):
        code = came[sender].astype(jnp.int32).astype(F32)
        logits = logits + code * (code[-1:] * (REACH / TOP / TOP))
    kind = lax.broadcasted_iota(jnp.int32, logits.shape, 0)
    logits = jnp.where(kind == classes - 1, 0.0, logits)
    exponent = jnp.exp(logits - jnp.max(logits, axis=0, keepdims=True))
    share = exponent / jnp.sum(exponent, axis=0, keepdims=True)
    shares[...] = share
    lines = own // LANES
    first = (lax.axis_index("c") * depth + lax.axis_index("z")) * lines
    label = jnp.concatenate([labels[pl.ds(first + line, 1), :] for line in range(lines)], axis=1)
    repeat(sent, (share - (label == kind).astype(F32)).astype(BF16))


def columns(came, rows):
    core = lax.axis_index("c")
    depth = came.shape[0]
    sums = []
    for owner in (core, 1 - core):
        first = owner * depth
        total = jnp.dot(came[0], rows[first], preferred_element_type=F32)
        for level in range(1, depth):
            total = total + jnp.dot(came[level], rows[first + level], preferred_element_type=F32)
        sums.append(total)
    return sums


def misfit_columns_kernel(ridge, came, rows, weights, part):
    own, far = columns(came, rows)
    width = own.shape[1]
    part[:, :width] = own + ridge * weights[...]
    part[:, width:] = far


def image_columns_kernel(came, rows, sent):
    repeat(sent, jnp.concatenate(columns(came, rows), axis=1).astype(BF16))


def pair_kernel(parts, sent):
    core = lax.axis_index("c")
    repeat(sent, parts[core] + turned(parts[1 - core]))


def turned(block):
    width = block.shape[1] // CORES
    return jnp.concatenate([block[:, width:], block[:, :width]], axis=1)


def arrived_pair(ref):
    core = lax.axis_index("c")
    near, far = ref[core].astype(F32), ref[1 - core].astype(F32)
    for row in range(1, ref.shape[0] // CORES):
        near = near + ref[row * CORES + core].astype(F32)
        far = far + ref[row * CORES + 1 - core].astype(F32)
    return near + turned(far)


def respond(vector, rows, depth):
    core = lax.axis_index("c")
    width = rows.shape[2]
    own, far = vector[:, :width].astype(BF16), vector[:, width:].astype(BF16)
    for level in range(depth):
        near = times_transposed(own, rows[core * depth + level])
        yield near + times_transposed(far, rows[(1 - core) * depth + level])


def gradient_kernel(users, came, rows, gradient, residual, sent):
    width = gradient.shape[1]
    value = arrived(came) / users
    gradient[...] = value[:, :width]
    residual[...] = -value
    for level, answer in enumerate(respond(-value, rows, sent.shape[0])):
        sent[level] = answer.astype(BF16)


def weigh_kernel(came, shares, count, response, sent):
    value = arrived(came)
    response[...] = value
    share = shares[...]
    repeat(sent, (count[...] * (share * (value - shares_sum(share, value)))).astype(BF16))


def image_kernel(sub_total, came, residual, rows, image, sent):
    start = residual[...]
    value = arrived_pair(came) / sub_total + RIDGE_WEIGHT * start
    image[...] = value
    _, classes, own = sent.shape
    lane = lax.broadcasted_iota(jnp.int32, (1, own), 1)
    line = jnp.zeros(lane.shape, F32)
    for which, product in enumerate((start * start, start * value, value * value)):
        left = whole(product)
        for piece in range(PIECES):
            head = left.astype(BF16).astype(F32)
            line = jnp.where(lane == which * PIECES + piece, head, line)
            left = left - head
    last = lax.broadcasted_iota(jnp.int32, (classes, own), 0) == classes - 1
    for level, answer in enumerate(respond(value, rows, sent.shape[0])):
        sent[level] = jnp.where(last, line, answer - answer[-1:]).astype(BF16)


def direction_kernel(came, response, shares, count, residual, image, base, direction, sent):
    got = arrived(came)
    classes, own = got.shape
    width = base.shape[1]
    line = got[-1:]
    lane = lax.broadcasted_iota(jnp.int32, line.shape, 1)

    def scalar(which):
        pieces = jnp.logical_and(lane >= which * PIECES, lane < (which + 1) * PIECES)
        return jnp.sum(jnp.where(pieces, line, 0.0), axis=1, keepdims=True)

    norm, curve, image_norm = scalar(0), scalar(1), scalar(2)
    step = norm / curve
    beta = jnp.maximum(image_norm / curve * step - 1.0, 0.0)
    start = residual[...]
    after = start - step * image[...]
    second = after + beta * start
    base[...] = step * start[:, :width]
    direction[...] = second[:, :width]
    image_response = jnp.where(lax.broadcasted_iota(jnp.int32, got.shape, 0) == classes - 1, 0.0, got)
    share = shares[...]
    value = (1.0 + beta) * response[...] - step * image_response
    centred = value - shares_sum(share, value)
    lane = lax.broadcasted_iota(jnp.int32, (1, LANES), 1)
    line = jnp.where(lane == 0, whole(after * after), whole(second * second))
    line = jnp.where(lane < 2, line, whole(count[...] * (share * (centred * centred))))
    repeat(sent, line)


def relay_kernel(came, sent):
    repeat(sent, arrived(came))


def step_kernel(sub_total, copies, came, base, direction, newton_step):
    line = arrived(came)
    norm, square, spread = line[:, 0:1] / copies, line[:, 1:2] / copies, line[:, 2:3]
    curve = spread / sub_total + RIDGE_WEIGHT * square
    newton_step[...] = base[...] + norm / curve * direction[...]


def swap(block, axis):
    return lax.all_to_all(block, axis, 0, 0, tiled=True)


def array(*shape, dtype=F32):
    return jax.ShapeDtypeStruct(shape, dtype)


def body(covariates, labels, weights, sample_index):
    user_rows, width = covariates.shape
    classes = weights.shape[0]
    row_count, depth = lax.axis_size("row"), lax.axis_size("z")
    users = user_rows * row_count
    sub_total = sample_index.shape[0] * row_count
    own = user_rows // CORES // depth
    wide = CORES * width
    blocks = (depth, classes, own)
    rows = covariates.reshape(CORES * depth, own, width)
    labels = labels.reshape(-1, LANES)
    sample_index = sample_index.reshape(-1, LANES)

    pair_rows = swap(rows, "c")
    pair_weights = lax.all_gather(weights, "c", axis=0)
    count = kernel_call(functools.partial(count_kernel, user_rows, depth), array(1, own), sample_index)
    sent = kernel_call(code_kernel, array(*blocks, dtype=jnp.int16), pair_weights, pair_rows)
    shares, sent = kernel_call(
        misfit_kernel, (array(classes, own), array(*blocks, dtype=BF16)), swap(sent, "z"), labels
    )

    ridge = RIDGE_WEIGHT * users / row_count
    part = kernel_call(
        functools.partial(misfit_columns_kernel, ridge), array(classes, wide), swap(sent, "z"), pair_rows, weights
    )
    parts = lax.all_gather(part, "c", axis=0)
    sent = kernel_call(pair_kernel, array(row_count, classes, wide), parts)
    gradient, residual, sent = kernel_call(
        functools.partial(gradient_kernel, users),
        (array(classes, width), array(classes, wide), array(*blocks, dtype=BF16)),
        swap(sent, "row"), pair_rows,
    )
    response, sent = kernel_call(
        weigh_kernel, (array(classes, own), array(*blocks, dtype=BF16)), swap(sent, "z"), shares, count
    )
    sent = kernel_call(
        image_columns_kernel, array(row_count * CORES, classes, wide, dtype=BF16), swap(sent, "z"), pair_rows
    )
    image, sent = kernel_call(
        functools.partial(image_kernel, sub_total),
        (array(classes, wide), array(*blocks, dtype=BF16)),
        swap(sent, ("row", "c")), residual, pair_rows,
    )
    base, direction, sent = kernel_call(
        direction_kernel,
        (array(classes, width), array(classes, width), array(depth, 1, LANES)),
        swap(sent, "z"), response, shares, count, residual, image,
    )
    sent = kernel_call(relay_kernel, array(row_count * CORES, 1, LANES), swap(sent, "z"))
    newton_step = kernel_call(
        functools.partial(step_kernel, sub_total, row_count * CORES),
        array(classes, width),
        swap(sent, ("row", "c")), base, direction,
    )
    return gradient, newton_step


def solution(mesh):
    rows, cols = mesh.devices.shape
    fine = Mesh(mesh.devices.reshape(rows, cols // CORES, CORES), ("row", "z", "c"))
    in_specs = (P("row", ("z", "c")), P("row"), P(None, ("z", "c")), P("row"))
    out_specs = (P(None, ("z", "c")), P(None, ("z", "c")))
    return jax.shard_map(body, mesh=fine, in_specs=in_specs, out_specs=out_specs, check_vma=False)
```

```python
import functools

import jax
import jax.numpy as jnp
from jax import lax
from jax.experimental import pallas as pl
from jax.experimental.pallas import tpu as pltpu
from jax.sharding import Mesh, PartitionSpec as P

RIDGE_WEIGHT = 0.004
F32, BF16 = jnp.float32, jnp.bfloat16
LANES, SUBLANES = 128, 8
PIECES = 3
CORES = 2
GROUPS = 4
TOP, REACH = 32767.0, 768.0


def kernel_call(body, out_shape, *operands):
    return pl.pallas_call(
        body,
        out_shape=out_shape,
        in_specs=[pl.BlockSpec(memory_space=pltpu.VMEM)] * len(operands),
        out_specs=jax.tree.map(lambda _: pl.BlockSpec(memory_space=pltpu.VMEM), out_shape),
        compiler_params=pltpu.CompilerParams(vmem_limit_bytes=24 * 1024 * 1024),
    )(*operands)


def times_transposed(left, right):
    return lax.dot_general(left, right, (((1,), (1,)), ((), ())), preferred_element_type=F32)


def arrived(ref):
    total = ref[0].astype(F32)
    for sender in range(1, ref.shape[0]):
        total = total + ref[sender].astype(F32)
    return total


def repeat(ref, block):
    for receiver in range(ref.shape[0]):
        ref[receiver] = block


def shares_sum(shares, block):
    return jnp.sum(shares * block, axis=0, keepdims=True)


def whole(block):
    return jnp.sum(jnp.sum(block, axis=1, keepdims=True), axis=0, keepdims=True)


def parcel_kernel(weights, rows_hbm, parcel_hbm, rounded, weights_sem, row_sems):
    half = rows_hbm.shape[0] // CORES
    first = (1 - lax.axis_index("c")) * half
    step = half // GROUPS
    copies = []
    for group in range(GROUPS):
        source = rows_hbm.at[pl.ds(first + group * step, step)]
        target = parcel_hbm.at[pl.ds(group * step, step)]
        copies.append(pltpu.make_async_copy(source, target, row_sems.at[group]))
        copies[-1].start()
    rounded[...] = weights[...].astype(BF16)
    copies.append(pltpu.make_async_copy(rounded, parcel_hbm.at[pl.ds(half, weights.shape[0])], weights_sem))
    copies[-1].start()
    for copy in copies:
        copy.wait()


def keep_kernel(weights, rows, index, mine, count):
    depth, _, own = mine.shape
    core = lax.axis_index("c")
    place = core * depth + lax.axis_index("z")
    rounded = weights[...].astype(BF16)
    for level in range(depth):
        mine[level] = times_transposed(rounded, rows[core * depth + level])
    offset = index[...] - (lax.axis_index("row") * (CORES * depth * own) + place * own)
    low, high = offset & (LANES - 1), offset >> 7
    low_place = lax.broadcasted_iota(jnp.int32, (LANES, LANES), 0)
    high_place = lax.broadcasted_iota(jnp.int32, (SUBLANES, LANES), 0)
    drawn = jnp.zeros((SUBLANES, LANES), F32)
    for line in range(index.shape[0]):
        is_low = (low[line : line + 1] == low_place).astype(F32).astype(BF16)
        is_high = (high[line : line + 1] == high_place).astype(F32).astype(BF16)
        drawn = drawn + times_transposed(is_high, is_low)
    for part in range(own // LANES):
        count[:, part * LANES : (part + 1) * LANES] = drawn[part : part + 1]


def code_kernel(mine, parcel, sent):
    depth, classes, own = mine.shape
    rounded = parcel[depth * own :]
    for level in range(depth):
        value = mine[level] + times_transposed(rounded, parcel[level * own : (level + 1) * own])
        value = value - value[-1:]
        largest = jnp.max(jnp.abs(value), axis=0, keepdims=True)
        scale = jnp.minimum(jnp.floor(largest * (TOP / REACH)) + 1.0, TOP)
        code = jnp.floor(value * (TOP * TOP / REACH / scale) + 0.5)
        code = jnp.clip(code, -TOP, TOP)
        last = lax.broadcasted_iota(jnp.int32, value.shape, 0) == classes - 1
        sent[level] = jnp.where(last, scale, code).astype(jnp.int32).astype(jnp.int16)


def misfit_kernel(came, labels, shares, sent):
    depth, classes, own = came.shape
    logits = jnp.zeros((classes, own), F32)
    for sender in range(depth):
        code = came[sender].astype(jnp.int32).astype(F32)
        logits = logits + code * (code[-1:] * (REACH / TOP / TOP))
    kind = lax.broadcasted_iota(jnp.int32, logits.shape, 0)
    logits = jnp.where(kind == classes - 1, 0.0, logits)
    exponent = jnp.exp(logits - jnp.max(logits, axis=0, keepdims=True))
    share = exponent / jnp.sum(exponent, axis=0, keepdims=True)
    shares[...] = share
    lines = own // LANES
    first = (lax.axis_index("c") * depth + lax.axis_index("z")) * lines
    label = jnp.concatenate([labels[pl.ds(first + line, 1), :] for line in range(lines)], axis=1)
    repeat(sent, (share - (label == kind).astype(F32)).astype(BF16))


def columns(came, rows, parcel):
    core = lax.axis_index("c")
    depth, _, own = came.shape
    near = jnp.dot(came[0], rows[core * depth], preferred_element_type=F32)
    far = jnp.dot(came[0], parcel[:own], preferred_element_type=F32)
    for level in range(1, depth):
        near = near + jnp.dot(came[level], rows[core * depth + level], preferred_element_type=F32)
        far = far + jnp.dot(came[level], parcel[level * own : (level + 1) * own], preferred_element_type=F32)
    return near, far


def misfit_columns_kernel(ridge, came, rows, parcel, weights, part):
    own, far = columns(came, rows, parcel)
    width = own.shape[1]
    part[:, :width] = own + ridge * weights[...]
    part[:, width:] = far


def image_columns_kernel(came, rows, parcel, sent):
    repeat(sent, jnp.concatenate(columns(came, rows, parcel), axis=1).astype(BF16))


def pair_kernel(parts, sent):
    core = lax.axis_index("c")
    repeat(sent, parts[core] + turned(parts[1 - core]))


def turned(block):
    width = block.shape[1] // CORES
    return jnp.concatenate([block[:, width:], block[:, :width]], axis=1)


def arrived_pair(ref):
    core = lax.axis_index("c")
    near, far = ref[core].astype(F32), ref[1 - core].astype(F32)
    for row in range(1, ref.shape[0] // CORES):
        near = near + ref[row * CORES + core].astype(F32)
        far = far + ref[row * CORES + 1 - core].astype(F32)
    return near + turned(far)


def respond(vector, rows, parcel, depth):
    core = lax.axis_index("c")
    _, users, width = rows.shape
    own, far = vector[:, :width].astype(BF16), vector[:, width:].astype(BF16)
    for level in range(depth):
        near = times_transposed(own, rows[core * depth + level])
        yield near + times_transposed(far, parcel[level * users : (level + 1) * users])


def gradient_kernel(users, came, rows, parcel, residual, sent):
    value = arrived(came) / -users
    residual[...] = value
    for level, answer in enumerate(respond(value, rows, parcel, sent.shape[0])):
        sent[level] = answer.astype(BF16)


def weigh_kernel(came, shares, count, response, sent):
    value = arrived(came)
    response[...] = value
    share = shares[...]
    repeat(sent, (count[...] * (share * (value - shares_sum(share, value)))).astype(BF16))


def image_kernel(sub_total, came, residual, rows, parcel, image, sent):
    start = residual[...]
    value = arrived_pair(came) / sub_total + RIDGE_WEIGHT * start
    image[...] = value
    _, classes, own = sent.shape
    lane = lax.broadcasted_iota(jnp.int32, (1, own), 1)
    line = jnp.zeros(lane.shape, F32)
    for which, product in enumerate((start * start, start * value, value * value)):
        left = whole(product)
        for piece in range(PIECES):
            head = left.astype(BF16).astype(F32)
            line = jnp.where(lane == which * PIECES + piece, head, line)
            left = left - head
    last = lax.broadcasted_iota(jnp.int32, (classes, own), 0) == classes - 1
    for level, answer in enumerate(respond(value, rows, parcel, sent.shape[0])):
        sent[level] = jnp.where(last, line, answer - answer[-1:]).astype(BF16)


def direction_kernel(came, response, shares, count, residual, image, base, direction, sent):
    got = arrived(came)
    classes, own = got.shape
    width = base.shape[1]
    line = got[-1:]
    lane = lax.broadcasted_iota(jnp.int32, line.shape, 1)

    def scalar(which):
        pieces = jnp.logical_and(lane >= which * PIECES, lane < (which + 1) * PIECES)
        return jnp.sum(jnp.where(pieces, line, 0.0), axis=1, keepdims=True)

    norm, curve, image_norm = scalar(0), scalar(1), scalar(2)
    step = norm / curve
    beta = jnp.maximum(image_norm / curve * step - 1.0, 0.0)
    start = residual[...]
    after = start - step * image[...]
    second = after + beta * start
    base[...] = step * start[:, :width]
    direction[...] = second[:, :width]
    image_response = jnp.where(lax.broadcasted_iota(jnp.int32, got.shape, 0) == classes - 1, 0.0, got)
    share = shares[...]
    value = (1.0 + beta) * response[...] - step * image_response
    centred = value - shares_sum(share, value)
    lane = lax.broadcasted_iota(jnp.int32, (1, LANES), 1)
    line = jnp.where(lane == 0, whole(after * after), whole(second * second))
    line = jnp.where(lane < 2, line, whole(count[...] * (share * (centred * centred))))
    repeat(sent, line)


def relay_kernel(came, sent):
    repeat(sent, arrived(came))


def step_kernel(sub_total, copies, came, residual, base, direction, gradient, newton_step):
    gradient[...] = -residual[:, : gradient.shape[1]]
    line = arrived(came)
    norm, square, spread = line[:, 0:1] / copies, line[:, 1:2] / copies, line[:, 2:3]
    curve = spread / sub_total + RIDGE_WEIGHT * square
    newton_step[...] = base[...] + norm / curve * direction[...]


def swap(block, axis):
    return lax.all_to_all(block, axis, 0, 0, tiled=True)


def array(*shape, dtype=F32):
    return jax.ShapeDtypeStruct(shape, dtype)


def body(covariates, labels, weights, sample_index):
    user_rows, width = covariates.shape
    classes = weights.shape[0]
    row_count, depth = lax.axis_size("row"), lax.axis_size("z")
    users = user_rows * row_count
    sub_total = sample_index.shape[0] * row_count
    own = user_rows // CORES // depth
    wide = CORES * width
    blocks = (depth, classes, own)
    rows = covariates.reshape(CORES * depth, own, width)
    labels = labels.reshape(-1, LANES)
    sample_index = sample_index.reshape(-1, LANES)

    parcel = pl.pallas_call(
        parcel_kernel,
        out_shape=array(user_rows // CORES + classes, width, dtype=BF16),
        in_specs=[pl.BlockSpec(memory_space=pltpu.VMEM), pl.BlockSpec(memory_space=pl.ANY)],
        out_specs=pl.BlockSpec(memory_space=pl.ANY),
        scratch_shapes=[
            pltpu.VMEM(weights.shape, BF16),
            pltpu.SemaphoreType.DMA,
            pltpu.SemaphoreType.DMA((GROUPS,)),
        ],
    )(weights, covariates)
    parcel = lax.ppermute(parcel, "c", [(0, 1), (1, 0)])
    mine, count = kernel_call(keep_kernel, (array(*blocks), array(1, own)), weights, rows, sample_index)
    sent = kernel_call(code_kernel, array(*blocks, dtype=jnp.int16), mine, parcel)
    shares, sent = kernel_call(
        misfit_kernel, (array(classes, own), array(*blocks, dtype=BF16)), swap(sent, "z"), labels
    )

    ridge = RIDGE_WEIGHT * users / row_count
    part = kernel_call(
        functools.partial(misfit_columns_kernel, ridge), array(classes, wide), swap(sent, "z"), rows, parcel, weights
    )
    parts = lax.all_gather(part, "c", axis=0)
    sent = kernel_call(pair_kernel, array(row_count, classes, wide), parts)
    residual, sent = kernel_call(
        functools.partial(gradient_kernel, users),
        (array(classes, wide), array(*blocks, dtype=BF16)),
        swap(sent, "row"), rows, parcel,
    )
    response, sent = kernel_call(
        weigh_kernel, (array(classes, own), array(*blocks, dtype=BF16)), swap(sent, "z"), shares, count
    )
    sent = kernel_call(
        image_columns_kernel, array(row_count * CORES, classes, wide, dtype=BF16), swap(sent, "z"), rows, parcel
    )
    image, sent = kernel_call(
        functools.partial(image_kernel, sub_total),
        (array(classes, wide), array(*blocks, dtype=BF16)),
        swap(sent, ("row", "c")), residual, rows, parcel,
    )
    base, direction, sent = kernel_call(
        direction_kernel,
        (array(classes, width), array(classes, width), array(depth, 1, LANES)),
        swap(sent, "z"), response, shares, count, residual, image,
    )
    sent = kernel_call(relay_kernel, array(row_count * CORES, 1, LANES), swap(sent, "z"))
    return kernel_call(
        functools.partial(step_kernel, sub_total, row_count * CORES),
        (array(classes, width), array(classes, width)),
        swap(sent, ("row", "c")), residual, base, direction,
    )


def solution(mesh):
    rows, cols = mesh.devices.shape
    fine = Mesh(mesh.devices.reshape(rows, cols // CORES, CORES), ("row", "z", "c"))
    in_specs = (P("row", ("z", "c")), P("row"), P(None, ("z", "c")), P("row"))
    out_specs = (P(None, ("z", "c")), P(None, ("z", "c")))
    return jax.shard_map(body, mesh=fine, in_specs=in_specs, out_specs=out_specs, check_vma=False)
```

```python
import functools

import jax
import jax.numpy as jnp
from jax import lax
from jax.experimental import pallas as pl
from jax.experimental.pallas import tpu as pltpu
from jax.sharding import Mesh, PartitionSpec as P

RIDGE_WEIGHT = 0.004
F32, BF16 = jnp.float32, jnp.bfloat16
LANES, SUBLANES = 128, 8
PIECES = 3
CORES = 2
GROUPS = 4
TOP, REACH = 32767.0, 768.0


def kernel_call(body, out_shape, *operands):
    return pl.pallas_call(
        body,
        out_shape=out_shape,
        in_specs=[pl.BlockSpec(memory_space=pltpu.VMEM)] * len(operands),
        out_specs=jax.tree.map(lambda _: pl.BlockSpec(memory_space=pltpu.VMEM), out_shape),
        compiler_params=pltpu.CompilerParams(vmem_limit_bytes=24 * 1024 * 1024),
    )(*operands)


def times_transposed(left, right):
    return lax.dot_general(left, right, (((1,), (1,)), ((), ())), preferred_element_type=F32)


def arrived(ref):
    total = ref[0].astype(F32)
    for sender in range(1, ref.shape[0]):
        total = total + ref[sender].astype(F32)
    return total


def repeat(ref, block):
    for receiver in range(ref.shape[0]):
        ref[receiver] = block


def shares_sum(shares, block):
    return jnp.sum(shares * block, axis=0, keepdims=True)


def whole(block):
    return jnp.sum(jnp.sum(block, axis=1, keepdims=True), axis=0, keepdims=True)


def parcel_kernel(weights, rows_hbm, parcel_hbm, rounded, staged, weights_sem, in_sems, out_sems):
    half = staged.shape[0]
    first = (1 - lax.axis_index("c")) * half
    step = half // GROUPS
    ins, outs = [], []
    for group in range(GROUPS):
        here = staged.at[pl.ds(group * step, step)]
        ins.append(
            pltpu.make_async_copy(rows_hbm.at[pl.ds(first + group * step, step)], here, in_sems.at[group])
        )
        outs.append(pltpu.make_async_copy(here, parcel_hbm.at[pl.ds(group * step, step)], out_sems.at[group]))
        ins[-1].start()
    rounded[...] = weights[...].astype(BF16)
    outs.append(pltpu.make_async_copy(rounded, parcel_hbm.at[pl.ds(half, weights.shape[0])], weights_sem))
    outs[-1].start()
    for group in range(GROUPS):
        ins[group].wait()
        outs[group].start()
    for copy in outs:
        copy.wait()


def keep_kernel(weights, rows, index, mine, count):
    depth, _, own = mine.shape
    core = lax.axis_index("c")
    place = core * depth + lax.axis_index("z")
    rounded = weights[...].astype(BF16)
    for level in range(depth):
        mine[level] = times_transposed(rounded, rows[core * depth + level])
    offset = index[...] - (lax.axis_index("row") * (CORES * depth * own) + place * own)
    low, high = offset & (LANES - 1), offset >> 7
    low_place = lax.broadcasted_iota(jnp.int32, (LANES, LANES), 0)
    high_place = lax.broadcasted_iota(jnp.int32, (SUBLANES, LANES), 0)
    drawn = jnp.zeros((SUBLANES, LANES), F32)
    for line in range(index.shape[0]):
        is_low = (low[line : line + 1] == low_place).astype(F32).astype(BF16)
        is_high = (high[line : line + 1] == high_place).astype(F32).astype(BF16)
        drawn = drawn + times_transposed(is_high, is_low)
    for part in range(own // LANES):
        count[:, part * LANES : (part + 1) * LANES] = drawn[part : part + 1]


def code_kernel(mine, parcel, sent):
    depth, classes, own = mine.shape
    rounded = parcel[depth * own :]
    for level in range(depth):
        value = mine[level] + times_transposed(rounded, parcel[level * own : (level + 1) * own])
        value = value - value[-1:]
        largest = jnp.max(jnp.abs(value), axis=0, keepdims=True)
        scale = jnp.minimum(jnp.floor(largest * (TOP / REACH)) + 1.0, TOP)
        code = jnp.floor(value * (TOP * TOP / REACH / scale) + 0.5)
        code = jnp.clip(code, -TOP, TOP)
        last = lax.broadcasted_iota(jnp.int32, value.shape, 0) == classes - 1
        sent[level] = jnp.where(last, scale, code).astype(jnp.int32).astype(jnp.int16)


def misfit_kernel(came, labels, shares, sent):
    depth, classes, own = came.shape
    logits = jnp.zeros((classes, own), F32)
    for sender in range(depth):
        code = came[sender].astype(jnp.int32).astype(F32)
        logits = logits + code * (code[-1:] * (REACH / TOP / TOP))
    kind = lax.broadcasted_iota(jnp.int32, logits.shape, 0)
    logits = jnp.where(kind == classes - 1, 0.0, logits)
    exponent = jnp.exp(logits - jnp.max(logits, axis=0, keepdims=True))
    share = exponent / jnp.sum(exponent, axis=0, keepdims=True)
    shares[...] = share
    lines = own // LANES
    first = (lax.axis_index("c") * depth + lax.axis_index("z")) * lines
    label = jnp.concatenate([labels[pl.ds(first + line, 1), :] for line in range(lines)], axis=1)
    repeat(sent, (share - (label == kind).astype(F32)).astype(BF16))


def columns(came, rows, parcel):
    core = lax.axis_index("c")
    depth, _, own = came.shape
    near = jnp.dot(came[0], rows[core * depth], preferred_element_type=F32)
    far = jnp.dot(came[0], parcel[:own], preferred_element_type=F32)
    for level in range(1, depth):
        near = near + jnp.dot(came[level], rows[core * depth + level], preferred_element_type=F32)
        far = far + jnp.dot(came[level], parcel[level * own : (level + 1) * own], preferred_element_type=F32)
    return near, far


def misfit_columns_kernel(ridge, came, rows, parcel, weights, part):
    own, far = columns(came, rows, parcel)
    width = own.shape[1]
    part[:, :width] = own + ridge * weights[...]
    part[:, width:] = far


def image_columns_kernel(came, rows, parcel, sent):
    repeat(sent, jnp.concatenate(columns(came, rows, parcel), axis=1).astype(BF16))


def pair_kernel(parts, sent):
    core = lax.axis_index("c")
    repeat(sent, parts[core] + turned(parts[1 - core]))


def turned(block):
    width = block.shape[1] // CORES
    return jnp.concatenate([block[:, width:], block[:, :width]], axis=1)


def arrived_pair(ref):
    core = lax.axis_index("c")
    near, far = ref[core].astype(F32), ref[1 - core].astype(F32)
    for row in range(1, ref.shape[0] // CORES):
        near = near + ref[row * CORES + core].astype(F32)
        far = far + ref[row * CORES + 1 - core].astype(F32)
    return near + turned(far)


def respond(vector, rows, parcel, depth):
    core = lax.axis_index("c")
    _, users, width = rows.shape
    own, far = vector[:, :width].astype(BF16), vector[:, width:].astype(BF16)
    for level in range(depth):
        near = times_transposed(own, rows[core * depth + level])
        yield near + times_transposed(far, parcel[level * users : (level + 1) * users])


def gradient_kernel(users, came, rows, parcel, residual, sent):
    value = arrived(came) / -users
    residual[...] = value
    for level, answer in enumerate(respond(value, rows, parcel, sent.shape[0])):
        sent[level] = answer.astype(BF16)


def weigh_kernel(came, shares, count, response, sent):
    value = arrived(came)
    response[...] = value
    share = shares[...]
    repeat(sent, (count[...] * (share * (value - shares_sum(share, value)))).astype(BF16))


def image_kernel(sub_total, came, residual, rows, parcel, image, sent):
    start = residual[...]
    value = arrived_pair(came) / sub_total + RIDGE_WEIGHT * start
    image[...] = value
    _, classes, own = sent.shape
    lane = lax.broadcasted_iota(jnp.int32, (1, own), 1)
    line = jnp.zeros(lane.shape, F32)
    for which, product in enumerate((start * start, start * value, value * value)):
        left = whole(product)
        for piece in range(PIECES):
            head = left.astype(BF16).astype(F32)
            line = jnp.where(lane == which * PIECES + piece, head, line)
            left = left - head
    last = lax.broadcasted_iota(jnp.int32, (classes, own), 0) == classes - 1
    for level, answer in enumerate(respond(value, rows, parcel, sent.shape[0])):
        sent[level] = jnp.where(last, line, answer - answer[-1:]).astype(BF16)


def direction_kernel(came, response, shares, count, residual, image, base, direction, sent):
    got = arrived(came)
    classes, own = got.shape
    width = base.shape[1]
    line = got[-1:]
    lane = lax.broadcasted_iota(jnp.int32, line.shape, 1)

    def scalar(which):
        pieces = jnp.logical_and(lane >= which * PIECES, lane < (which + 1) * PIECES)
        return jnp.sum(jnp.where(pieces, line, 0.0), axis=1, keepdims=True)

    norm, curve, image_norm = scalar(0), scalar(1), scalar(2)
    step = norm / curve
    beta = jnp.maximum(image_norm / curve * step - 1.0, 0.0)
    start = residual[...]
    after = start - step * image[...]
    second = after + beta * start
    base[...] = step * start[:, :width]
    direction[...] = second[:, :width]
    image_response = jnp.where(lax.broadcasted_iota(jnp.int32, got.shape, 0) == classes - 1, 0.0, got)
    share = shares[...]
    value = (1.0 + beta) * response[...] - step * image_response
    centred = value - shares_sum(share, value)
    lane = lax.broadcasted_iota(jnp.int32, (1, LANES), 1)
    line = jnp.where(lane == 0, whole(after * after), whole(second * second))
    line = jnp.where(lane < 2, line, whole(count[...] * (share * (centred * centred))))
    repeat(sent, line)


def relay_kernel(came, sent):
    repeat(sent, arrived(came))


def step_kernel(sub_total, copies, came, residual, base, direction, gradient, newton_step):
    gradient[...] = -residual[:, : gradient.shape[1]]
    line = arrived(came)
    norm, square, spread = line[:, 0:1] / copies, line[:, 1:2] / copies, line[:, 2:3]
    curve = spread / sub_total + RIDGE_WEIGHT * square
    newton_step[...] = base[...] + norm / curve * direction[...]


def swap(block, axis):
    return lax.all_to_all(block, axis, 0, 0, tiled=True)


def array(*shape, dtype=F32):
    return jax.ShapeDtypeStruct(shape, dtype)


def body(covariates, labels, weights, sample_index):
    user_rows, width = covariates.shape
    classes = weights.shape[0]
    row_count, depth = lax.axis_size("row"), lax.axis_size("z")
    users = user_rows * row_count
    sub_total = sample_index.shape[0] * row_count
    own = user_rows // CORES // depth
    wide = CORES * width
    blocks = (depth, classes, own)
    rows = covariates.reshape(CORES * depth, own, width)
    labels = labels.reshape(-1, LANES)
    sample_index = sample_index.reshape(-1, LANES)

    parcel = pl.pallas_call(
        parcel_kernel,
        out_shape=array(user_rows // CORES + classes, width, dtype=BF16),
        in_specs=[pl.BlockSpec(memory_space=pltpu.VMEM), pl.BlockSpec(memory_space=pl.ANY)],
        out_specs=pl.BlockSpec(memory_space=pl.ANY),
        scratch_shapes=[
            pltpu.VMEM(weights.shape, BF16),
            pltpu.VMEM((user_rows // CORES, width), BF16),
            pltpu.SemaphoreType.DMA,
            pltpu.SemaphoreType.DMA((GROUPS,)),
            pltpu.SemaphoreType.DMA((GROUPS,)),
        ],
    )(weights, covariates)
    parcel = lax.ppermute(parcel, "c", [(0, 1), (1, 0)])
    mine, count = kernel_call(keep_kernel, (array(*blocks), array(1, own)), weights, rows, sample_index)
    sent = kernel_call(code_kernel, array(*blocks, dtype=jnp.int16), mine, parcel)
    shares, sent = kernel_call(
        misfit_kernel, (array(classes, own), array(*blocks, dtype=BF16)), swap(sent, "z"), labels
    )

    ridge = RIDGE_WEIGHT * users / row_count
    part = kernel_call(
        functools.partial(misfit_columns_kernel, ridge), array(classes, wide), swap(sent, "z"), rows, parcel, weights
    )
    parts = lax.all_gather(part, "c", axis=0)
    sent = kernel_call(pair_kernel, array(row_count, classes, wide), parts)
    residual, sent = kernel_call(
        functools.partial(gradient_kernel, users),
        (array(classes, wide), array(*blocks, dtype=BF16)),
        swap(sent, "row"), rows, parcel,
    )
    response, sent = kernel_call(
        weigh_kernel, (array(classes, own), array(*blocks, dtype=BF16)), swap(sent, "z"), shares, count
    )
    sent = kernel_call(
        image_columns_kernel, array(row_count * CORES, classes, wide, dtype=BF16), swap(sent, "z"), rows, parcel
    )
    image, sent = kernel_call(
        functools.partial(image_kernel, sub_total),
        (array(classes, wide), array(*blocks, dtype=BF16)),
        swap(sent, ("row", "c")), residual, rows, parcel,
    )
    base, direction, sent = kernel_call(
        direction_kernel,
        (array(classes, width), array(classes, width), array(depth, 1, LANES)),
        swap(sent, "z"), response, shares, count, residual, image,
    )
    sent = kernel_call(relay_kernel, array(row_count * CORES, 1, LANES), swap(sent, "z"))
    return kernel_call(
        functools.partial(step_kernel, sub_total, row_count * CORES),
        (array(classes, width), array(classes, width)),
        swap(sent, ("row", "c")), residual, base, direction,
    )


def solution(mesh):
    rows, cols = mesh.devices.shape
    fine = Mesh(mesh.devices.reshape(rows, cols // CORES, CORES), ("row", "z", "c"))
    in_specs = (P("row", ("z", "c")), P("row"), P(None, ("z", "c")), P("row"))
    out_specs = (P(None, ("z", "c")), P(None, ("z", "c")))
    return jax.shard_map(body, mesh=fine, in_specs=in_specs, out_specs=out_specs, check_vma=False)
```

```python
import functools

import jax
import jax.numpy as jnp
from jax import lax
from jax.experimental import pallas as pl
from jax.experimental.pallas import tpu as pltpu
from jax.sharding import Mesh, PartitionSpec as P

RIDGE_WEIGHT = 0.004
F32, BF16 = jnp.float32, jnp.bfloat16
LANES, SUBLANES = 128, 8
PIECES = 3
CORES = 2
LIMIT = 24 * 1024 * 1024
TOP, REACH = 32767.0, 768.0


def kernel_call(body, out_shape, *operands):
    return pl.pallas_call(
        body,
        out_shape=out_shape,
        in_specs=[pl.BlockSpec(memory_space=pltpu.VMEM)] * len(operands),
        out_specs=jax.tree.map(lambda _: pl.BlockSpec(memory_space=pltpu.VMEM), out_shape),
        compiler_params=pltpu.CompilerParams(vmem_limit_bytes=LIMIT),
    )(*operands)


def times_transposed(left, right):
    return lax.dot_general(left, right, (((1,), (1,)), ((), ())), preferred_element_type=F32)


def arrived(ref):
    total = ref[0].astype(F32)
    for sender in range(1, ref.shape[0]):
        total = total + ref[sender].astype(F32)
    return total


def repeat(ref, block):
    for receiver in range(ref.shape[0]):
        ref[receiver] = block


def shares_sum(shares, block):
    return jnp.sum(shares * block, axis=0, keepdims=True)


def whole(block):
    return jnp.sum(jnp.sum(block, axis=1, keepdims=True), axis=0, keepdims=True)


def round_kernel(weights, far, rounded):
    del far
    rounded[...] = weights[...].astype(BF16)


def keep_kernel(weights, rows, index, mine, count):
    depth, _, own = mine.shape
    core = lax.axis_index("c")
    place = core * depth + lax.axis_index("z")
    rounded = weights[...].astype(BF16)
    for level in range(depth):
        mine[level] = times_transposed(rounded, rows[core * depth + level])
    offset = index[...] - (lax.axis_index("row") * (CORES * depth * own) + place * own)
    low, high = offset & (LANES - 1), offset >> 7
    low_place = lax.broadcasted_iota(jnp.int32, (LANES, LANES), 0)
    high_place = lax.broadcasted_iota(jnp.int32, (SUBLANES, LANES), 0)
    drawn = jnp.zeros((SUBLANES, LANES), F32)
    for line in range(index.shape[0]):
        is_low = (low[line : line + 1] == low_place).astype(F32).astype(BF16)
        is_high = (high[line : line + 1] == high_place).astype(F32).astype(BF16)
        drawn = drawn + times_transposed(is_high, is_low)
    for part in range(own // LANES):
        count[:, part * LANES : (part + 1) * LANES] = drawn[part : part + 1]


def code_kernel(mine, parcel, sent):
    depth, classes, own = mine.shape
    rounded = parcel[depth * own :]
    for level in range(depth):
        value = mine[level] + times_transposed(rounded, parcel[level * own : (level + 1) * own])
        value = value - value[-1:]
        largest = jnp.max(jnp.abs(value), axis=0, keepdims=True)
        scale = jnp.minimum(jnp.floor(largest * (TOP / REACH)) + 1.0, TOP)
        code = jnp.floor(value * (TOP * TOP / REACH / scale) + 0.5)
        code = jnp.clip(code, -TOP, TOP)
        last = lax.broadcasted_iota(jnp.int32, value.shape, 0) == classes - 1
        sent[level] = jnp.where(last, scale, code).astype(jnp.int32).astype(jnp.int16)


def misfit_kernel(came, labels, shares, sent):
    depth, classes, own = came.shape
    logits = jnp.zeros((classes, own), F32)
    for sender in range(depth):
        code = came[sender].astype(jnp.int32).astype(F32)
        logits = logits + code * (code[-1:] * (REACH / TOP / TOP))
    kind = lax.broadcasted_iota(jnp.int32, logits.shape, 0)
    logits = jnp.where(kind == classes - 1, 0.0, logits)
    exponent = jnp.exp(logits - jnp.max(logits, axis=0, keepdims=True))
    share = exponent / jnp.sum(exponent, axis=0, keepdims=True)
    shares[...] = share
    lines = own // LANES
    first = (lax.axis_index("c") * depth + lax.axis_index("z")) * lines
    label = jnp.concatenate([labels[pl.ds(first + line, 1), :] for line in range(lines)], axis=1)
    repeat(sent, (share - (label == kind).astype(F32)).astype(BF16))


def columns(came, rows, parcel):
    core = lax.axis_index("c")
    depth, _, own = came.shape
    near = jnp.dot(came[0], rows[core * depth], preferred_element_type=F32)
    far = jnp.dot(came[0], parcel[:own], preferred_element_type=F32)
    for level in range(1, depth):
        near = near + jnp.dot(came[level], rows[core * depth + level], preferred_element_type=F32)
        far = far + jnp.dot(came[level], parcel[level * own : (level + 1) * own], preferred_element_type=F32)
    return near, far


def misfit_columns_kernel(ridge, came, rows, parcel, weights, part):
    own, far = columns(came, rows, parcel)
    width = own.shape[1]
    part[:, :width] = own + ridge * weights[...]
    part[:, width:] = far


def image_columns_kernel(came, rows, parcel, part):
    own, far = columns(came, rows, parcel)
    width = own.shape[1]
    part[:, :width] = own
    part[:, width:] = far


def pair_kernel(parts, sent):
    core = lax.axis_index("c")
    mine, far = parts[core], parts[1 - core]
    width = mine.shape[1] // CORES
    both = mine + jnp.concatenate([far[:, width:], far[:, :width]], axis=1)
    repeat(sent, both.astype(sent.dtype))


def respond(vector, rows, parcel, depth):
    core = lax.axis_index("c")
    _, users, width = rows.shape
    own, far = vector[:, :width].astype(BF16), vector[:, width:].astype(BF16)
    for level in range(depth):
        near = times_transposed(own, rows[core * depth + level])
        yield near + times_transposed(far, parcel[level * users : (level + 1) * users])


def gradient_kernel(users, came, rows, parcel, residual, sent):
    value = arrived(came) / -users
    residual[...] = value
    for level, answer in enumerate(respond(value, rows, parcel, sent.shape[0])):
        sent[level] = answer.astype(BF16)


def weigh_kernel(came, shares, count, response, sent):
    value = arrived(came)
    response[...] = value
    share = shares[...]
    repeat(sent, (count[...] * (share * (value - shares_sum(share, value)))).astype(BF16))


def image_kernel(sub_total, came, residual, rows, parcel, image, sent):
    start = residual[...]
    value = arrived(came) / sub_total + RIDGE_WEIGHT * start
    image[...] = value
    _, classes, own = sent.shape
    lane = lax.broadcasted_iota(jnp.int32, (1, own), 1)
    line = jnp.zeros(lane.shape, F32)
    for which, product in enumerate((start * start, start * value, value * value)):
        left = whole(product)
        for piece in range(PIECES):
            head = left.astype(BF16).astype(F32)
            line = jnp.where(lane == which * PIECES + piece, head, line)
            left = left - head
    last = lax.broadcasted_iota(jnp.int32, (classes, own), 0) == classes - 1
    for level, answer in enumerate(respond(value, rows, parcel, sent.shape[0])):
        sent[level] = jnp.where(last, line, answer - answer[-1:]).astype(BF16)


def direction_kernel(came, response, shares, count, residual, image, base, direction, sent):
    got = arrived(came)
    classes, own = got.shape
    width = base.shape[1]
    line = got[-1:]
    lane = lax.broadcasted_iota(jnp.int32, line.shape, 1)

    def scalar(which):
        pieces = jnp.logical_and(lane >= which * PIECES, lane < (which + 1) * PIECES)
        return jnp.sum(jnp.where(pieces, line, 0.0), axis=1, keepdims=True)

    norm, curve, image_norm = scalar(0), scalar(1), scalar(2)
    step = norm / curve
    beta = jnp.maximum(image_norm / curve * step - 1.0, 0.0)
    start = residual[...]
    after = start - step * image[...]
    second = after + beta * start
    base[...] = step * start[:, :width]
    direction[...] = second[:, :width]
    image_response = jnp.where(lax.broadcasted_iota(jnp.int32, got.shape, 0) == classes - 1, 0.0, got)
    share = shares[...]
    value = (1.0 + beta) * response[...] - step * image_response
    centred = value - shares_sum(share, value)
    lane = lax.broadcasted_iota(jnp.int32, (1, LANES), 1)
    line = jnp.where(lane == 0, whole(after * after), whole(second * second))
    line = jnp.where(lane < 2, line, whole(count[...] * (share * (centred * centred))))
    repeat(sent, line)


def relay_kernel(came, sent):
    repeat(sent, arrived(came))


def step_kernel(sub_total, copies, came, residual, base, direction, gradient, newton_step):
    gradient[...] = -residual[:, : gradient.shape[1]]
    line = arrived(came)
    norm, square, spread = line[:, 0:1] / copies, line[:, 1:2] / copies, line[:, 2:3]
    curve = spread / sub_total + RIDGE_WEIGHT * square
    newton_step[...] = base[...] + norm / curve * direction[...]


def swap(block, axis):
    return lax.all_to_all(block, axis, 0, 0, tiled=True)


def array(*shape, dtype=F32):
    return jax.ShapeDtypeStruct(shape, dtype)


def body(covariates, labels, weights, sample_index):
    user_rows, width = covariates.shape
    classes = weights.shape[0]
    row_count, depth = lax.axis_size("row"), lax.axis_size("z")
    users = user_rows * row_count
    sub_total = sample_index.shape[0] * row_count
    own = user_rows // CORES // depth
    wide = CORES * width
    blocks = (depth, classes, own)
    rows = covariates.reshape(CORES * depth, own, width)
    labels = labels.reshape(-1, LANES)
    sample_index = sample_index.reshape(-1, LANES)

    half = user_rows // CORES
    far = lax.dynamic_slice_in_dim(covariates, (1 - lax.axis_index("c")) * half, half, 0)
    rounded = pl.pallas_call(
        round_kernel,
        out_shape=array(classes, width, dtype=BF16),
        in_specs=[pl.BlockSpec(memory_space=pltpu.VMEM), pl.BlockSpec(memory_space=pl.ANY)],
        out_specs=pl.BlockSpec(memory_space=pltpu.VMEM),
        compiler_params=pltpu.CompilerParams(vmem_limit_bytes=LIMIT),
    )(weights, far)
    parcel = jnp.concatenate([far, rounded], axis=0)
    parcel = lax.ppermute(parcel, "c", [(0, 1), (1, 0)])
    mine, count = kernel_call(keep_kernel, (array(*blocks), array(1, own)), weights, rows, sample_index)
    sent = kernel_call(code_kernel, array(*blocks, dtype=jnp.int16), mine, parcel)
    shares, sent = kernel_call(
        misfit_kernel, (array(classes, own), array(*blocks, dtype=BF16)), swap(sent, "z"), labels
    )

    def add_pair(part, dtype):
        parts = lax.all_gather(part, "c", axis=0)
        return swap(kernel_call(pair_kernel, array(row_count, classes, wide, dtype=dtype), parts), "row")

    ridge = RIDGE_WEIGHT * users / row_count
    part = kernel_call(
        functools.partial(misfit_columns_kernel, ridge), array(classes, wide), swap(sent, "z"), rows, parcel, weights
    )
    residual, sent = kernel_call(
        functools.partial(gradient_kernel, users),
        (array(classes, wide), array(*blocks, dtype=BF16)),
        add_pair(part, F32), rows, parcel,
    )
    response, sent = kernel_call(
        weigh_kernel, (array(classes, own), array(*blocks, dtype=BF16)), swap(sent, "z"), shares, count
    )
    part = kernel_call(image_columns_kernel, array(classes, wide), swap(sent, "z"), rows, parcel)
    image, sent = kernel_call(
        functools.partial(image_kernel, sub_total),
        (array(classes, wide), array(*blocks, dtype=BF16)),
        add_pair(part, BF16), residual, rows, parcel,
    )
    base, direction, sent = kernel_call(
        direction_kernel,
        (array(classes, width), array(classes, width), array(depth, 1, LANES)),
        swap(sent, "z"), response, shares, count, residual, image,
    )
    sent = kernel_call(relay_kernel, array(row_count * CORES, 1, LANES), swap(sent, "z"))
    return kernel_call(
        functools.partial(step_kernel, sub_total, row_count * CORES),
        (array(classes, width), array(classes, width)),
        swap(sent, ("row", "c")), residual, base, direction,
    )


def solution(mesh):
    rows, cols = mesh.devices.shape
    fine = Mesh(mesh.devices.reshape(rows, cols // CORES, CORES), ("row", "z", "c"))
    in_specs = (P("row", ("z", "c")), P("row"), P(None, ("z", "c")), P("row"))
    out_specs = (P(None, ("z", "c")), P(None, ("z", "c")))
    return jax.shard_map(body, mesh=fine, in_specs=in_specs, out_specs=out_specs, check_vma=False)
```

```python
import functools

import jax
import jax.numpy as jnp
from jax import lax
from jax.experimental import pallas as pl
from jax.experimental.pallas import tpu as pltpu
from jax.sharding import Mesh, PartitionSpec as P

RIDGE_WEIGHT = 0.004
F32, BF16 = jnp.float32, jnp.bfloat16
LANES, SUBLANES = 128, 8
PIECES = 3
CORES = 2
LIMIT = 24 * 1024 * 1024
TOP, REACH = 32767.0, 768.0


def kernel_call(body, out_shape, *operands):
    return pl.pallas_call(
        body,
        out_shape=out_shape,
        in_specs=[pl.BlockSpec(memory_space=pltpu.VMEM)] * len(operands),
        out_specs=jax.tree.map(lambda _: pl.BlockSpec(memory_space=pltpu.VMEM), out_shape),
        compiler_params=pltpu.CompilerParams(vmem_limit_bytes=LIMIT),
    )(*operands)


def times_transposed(left, right):
    return lax.dot_general(left, right, (((1,), (1,)), ((), ())), preferred_element_type=F32)


def arrived(ref):
    total = ref[0].astype(F32)
    for sender in range(1, ref.shape[0]):
        total = total + ref[sender].astype(F32)
    return total


def repeat(ref, block):
    for receiver in range(ref.shape[0]):
        ref[receiver] = block


def shares_sum(shares, block):
    return jnp.sum(shares * block, axis=0, keepdims=True)


def whole(block):
    return jnp.sum(jnp.sum(block, axis=1, keepdims=True), axis=0, keepdims=True)


def round_kernel(weights, far, rounded):
    del far
    rounded[...] = weights[...].astype(BF16)


def keep_kernel(weights, rows, index, mine, count):
    depth, _, own = mine.shape
    core = lax.axis_index("c")
    place = core * depth + lax.axis_index("z")
    rounded = weights[...].astype(BF16)
    for level in range(depth):
        mine[level] = times_transposed(rounded, rows[core * depth + level])
    offset = index[...] - (lax.axis_index("row") * (CORES * depth * own) + place * own)
    low, high = offset & (LANES - 1), offset >> 7
    low_place = lax.broadcasted_iota(jnp.int32, (LANES, LANES), 0)
    high_place = lax.broadcasted_iota(jnp.int32, (SUBLANES, LANES), 0)
    drawn = jnp.zeros((SUBLANES, LANES), F32)
    for line in range(index.shape[0]):
        is_low = (low[line : line + 1] == low_place).astype(F32).astype(BF16)
        is_high = (high[line : line + 1] == high_place).astype(F32).astype(BF16)
        drawn = drawn + times_transposed(is_high, is_low)
    for part in range(own // LANES):
        count[:, part * LANES : (part + 1) * LANES] = drawn[part : part + 1]


def code_kernel(mine, parcel, sent):
    depth, classes, own = mine.shape
    rounded = parcel[depth * own :]
    for level in range(depth):
        value = mine[level] + times_transposed(rounded, parcel[level * own : (level + 1) * own])
        value = value - value[-1:]
        largest = jnp.max(jnp.abs(value), axis=0, keepdims=True)
        scale = jnp.minimum(jnp.floor(largest * (TOP / REACH)) + 1.0, TOP)
        code = jnp.floor(value * (TOP * TOP / REACH / scale) + 0.5)
        code = jnp.clip(code, -TOP, TOP)
        last = lax.broadcasted_iota(jnp.int32, value.shape, 0) == classes - 1
        sent[level] = jnp.where(last, scale, code).astype(jnp.int32).astype(jnp.int16)


def misfit_kernel(came, labels, shares, sent):
    depth, classes, own = came.shape
    logits = jnp.zeros((classes, own), F32)
    for sender in range(depth):
        code = came[sender].astype(jnp.int32).astype(F32)
        logits = logits + code * (code[-1:] * (REACH / TOP / TOP))
    kind = lax.broadcasted_iota(jnp.int32, logits.shape, 0)
    logits = jnp.where(kind == classes - 1, 0.0, logits)
    exponent = jnp.exp(logits - jnp.max(logits, axis=0, keepdims=True))
    share = exponent / jnp.sum(exponent, axis=0, keepdims=True)
    shares[...] = share
    lines = own // LANES
    first = (lax.axis_index("c") * depth + lax.axis_index("z")) * lines
    label = jnp.concatenate([labels[pl.ds(first + line, 1), :] for line in range(lines)], axis=1)
    repeat(sent, (share - (label == kind).astype(F32)).astype(BF16))


def columns(came, rows, parcel):
    core = lax.axis_index("c")
    depth, _, own = came.shape
    near = jnp.dot(came[0], rows[core * depth], preferred_element_type=F32)
    far = jnp.dot(came[0], parcel[:own], preferred_element_type=F32)
    for level in range(1, depth):
        near = near + jnp.dot(came[level], rows[core * depth + level], preferred_element_type=F32)
        far = far + jnp.dot(came[level], parcel[level * own : (level + 1) * own], preferred_element_type=F32)
    return near, far


def misfit_columns_kernel(ridge, came, rows, parcel, weights, part):
    own, far = columns(came, rows, parcel)
    width = own.shape[1]
    part[:, :width] = own + ridge * weights[...]
    part[:, width:] = far


def image_columns_kernel(came, rows, parcel, part):
    own, far = columns(came, rows, parcel)
    width = own.shape[1]
    part[:, :width] = own
    part[:, width:] = far


def pair_kernel(parts, sent):
    core = lax.axis_index("c")
    mine, far = parts[core], parts[1 - core]
    width = mine.shape[1] // CORES
    both = mine + jnp.concatenate([far[:, width:], far[:, :width]], axis=1)
    repeat(sent, both.astype(sent.dtype))


def respond(vector, rows, parcel, depth):
    core = lax.axis_index("c")
    _, users, width = rows.shape
    own, far = vector[:, :width].astype(BF16), vector[:, width:].astype(BF16)
    for level in range(depth):
        near = times_transposed(own, rows[core * depth + level])
        yield near + times_transposed(far, parcel[level * users : (level + 1) * users])


def gradient_kernel(users, came, rows, parcel, residual, sent):
    value = arrived(came) / -users
    residual[...] = value
    for level, answer in enumerate(respond(value, rows, parcel, sent.shape[0])):
        sent[level] = answer.astype(BF16)


def weigh_kernel(came, shares, count, response, sent):
    value = arrived(came)
    response[...] = value
    share = shares[...]
    repeat(sent, (count[...] * (share * (value - shares_sum(share, value)))).astype(BF16))


def image_kernel(sub_total, came, residual, rows, parcel, image, sent):
    start = residual[...]
    value = arrived(came) / sub_total + RIDGE_WEIGHT * start
    image[...] = value
    _, classes, own = sent.shape
    lane = lax.broadcasted_iota(jnp.int32, (1, own), 1)
    line = jnp.zeros(lane.shape, F32)
    for which, product in enumerate((start * start, start * value, value * value)):
        left = whole(product)
        for piece in range(PIECES):
            head = left.astype(BF16).astype(F32)
            line = jnp.where(lane == which * PIECES + piece, head, line)
            left = left - head
    last = lax.broadcasted_iota(jnp.int32, (classes, own), 0) == classes - 1
    for level, answer in enumerate(respond(value, rows, parcel, sent.shape[0])):
        sent[level] = jnp.where(last, line, answer - answer[-1:]).astype(BF16)


def direction_kernel(came, response, shares, count, residual, image, base, direction, sent):
    got = arrived(came)
    classes, own = got.shape
    width = base.shape[1]
    line = got[-1:]
    lane = lax.broadcasted_iota(jnp.int32, line.shape, 1)

    def scalar(which):
        pieces = jnp.logical_and(lane >= which * PIECES, lane < (which + 1) * PIECES)
        return jnp.sum(jnp.where(pieces, line, 0.0), axis=1, keepdims=True)

    norm, curve, image_norm = scalar(0), scalar(1), scalar(2)
    step = norm / curve
    beta = jnp.maximum(image_norm / curve * step - 1.0, 0.0)
    start = residual[...]
    after = start - step * image[...]
    second = after + beta * start
    base[...] = step * start[:, :width]
    direction[...] = second[:, :width]
    image_response = jnp.where(lax.broadcasted_iota(jnp.int32, got.shape, 0) == classes - 1, 0.0, got)
    share = shares[...]
    value = (1.0 + beta) * response[...] - step * image_response
    centred = value - shares_sum(share, value)
    lane = lax.broadcasted_iota(jnp.int32, (1, LANES), 1)
    line = jnp.where(lane == 0, whole(after * after), whole(second * second))
    line = jnp.where(lane < 2, line, whole(count[...] * (share * (centred * centred))))
    repeat(sent, line)


def relay_kernel(came, sent):
    repeat(sent, arrived(came))


def step_kernel(sub_total, copies, came, residual, base, direction, gradient, newton_step):
    gradient[...] = -residual[:, : gradient.shape[1]]
    line = arrived(came)
    norm, square, spread = line[:, 0:1] / copies, line[:, 1:2] / copies, line[:, 2:3]
    curve = spread / sub_total + RIDGE_WEIGHT * square
    newton_step[...] = base[...] + norm / curve * direction[...]


def swap(block, axis):
    return lax.all_to_all(block, axis, 0, 0, tiled=True)


def array(*shape, dtype=F32):
    return jax.ShapeDtypeStruct(shape, dtype)


def body(covariates, labels, weights, sample_index):
    user_rows, width = covariates.shape
    classes = weights.shape[0]
    row_count, depth = lax.axis_size("row"), lax.axis_size("z")
    users = user_rows * row_count
    sub_total = sample_index.shape[0] * row_count
    own = user_rows // CORES // depth
    wide = CORES * width
    blocks = (depth, classes, own)
    rows = covariates.reshape(CORES * depth, own, width)
    labels = labels.reshape(-1, LANES)
    sample_index = sample_index.reshape(-1, LANES)

    half = user_rows // CORES
    far = lax.dynamic_slice_in_dim(covariates, (1 - lax.axis_index("c")) * half, half, 0)
    rounded = pl.pallas_call(
        round_kernel,
        out_shape=array(classes, width, dtype=BF16),
        in_specs=[pl.BlockSpec(memory_space=pltpu.VMEM), pl.BlockSpec(memory_space=pl.ANY)],
        out_specs=pl.BlockSpec(memory_space=pltpu.VMEM),
        compiler_params=pltpu.CompilerParams(vmem_limit_bytes=LIMIT),
    )(weights, far)
    parcel = jnp.concatenate([far, rounded], axis=0)
    parcel = lax.ppermute(parcel, "c", [(0, 1), (1, 0)])
    mine, count = kernel_call(keep_kernel, (array(*blocks), array(1, own)), weights, rows, sample_index)
    sent = kernel_call(code_kernel, array(*blocks, dtype=jnp.int16), mine, parcel)
    shares, sent = kernel_call(
        misfit_kernel, (array(classes, own), array(*blocks, dtype=BF16)), swap(sent, "z"), labels
    )

    def add_pair(part, dtype):
        parts = lax.all_gather(part, "c", axis=0)
        return swap(kernel_call(pair_kernel, array(row_count, classes, wide, dtype=dtype), parts), "row")

    ridge = RIDGE_WEIGHT * users / row_count
    part = kernel_call(
        functools.partial(misfit_columns_kernel, ridge), array(classes, wide), swap(sent, "z"), rows, parcel, weights
    )
    residual, sent = kernel_call(
        functools.partial(gradient_kernel, users),
        (array(classes, wide), array(*blocks, dtype=BF16)),
        add_pair(part, F32), rows, parcel,
    )
    response, sent = kernel_call(
        weigh_kernel, (array(classes, own), array(*blocks, dtype=BF16)), swap(sent, "z"), shares, count
    )
    part = kernel_call(image_columns_kernel, array(classes, wide), swap(sent, "z"), rows, parcel)
    image, sent = kernel_call(
        functools.partial(image_kernel, sub_total),
        (array(classes, wide), array(*blocks, dtype=BF16)),
        add_pair(part, BF16), residual, rows, parcel,
    )
    base, direction, sent = kernel_call(
        direction_kernel,
        (array(classes, width), array(classes, width), array(depth * CORES, 1, LANES)),
        swap(sent, "z"), response, shares, count, residual, image,
    )
    sent = kernel_call(relay_kernel, array(row_count, 1, LANES), swap(sent, ("z", "c")))
    return kernel_call(
        functools.partial(step_kernel, sub_total, row_count * CORES),
        (array(classes, width), array(classes, width)),
        swap(sent, "row"), residual, base, direction,
    )


def solution(mesh):
    rows, cols = mesh.devices.shape
    fine = Mesh(mesh.devices.reshape(rows, cols // CORES, CORES), ("row", "z", "c"))
    in_specs = (P("row", ("z", "c")), P("row"), P(None, ("z", "c")), P("row"))
    out_specs = (P(None, ("z", "c")), P(None, ("z", "c")))
    return jax.shard_map(body, mesh=fine, in_specs=in_specs, out_specs=out_specs, check_vma=False)
```

```python
import functools

import jax
import jax.numpy as jnp
from jax import lax
from jax.experimental import pallas as pl
from jax.experimental.pallas import tpu as pltpu
from jax.sharding import Mesh, PartitionSpec as P

RIDGE_WEIGHT = 0.004
F32, BF16 = jnp.float32, jnp.bfloat16
LANES, SUBLANES = 128, 8
PIECES = 3
CORES = 2
LIMIT = 24 * 1024 * 1024
TOP, REACH = 32767.0, 768.0
STEPS, SMALLEST = 128.0, 1e-30


def kernel_call(body, out_shape, *operands):
    return pl.pallas_call(
        body,
        out_shape=out_shape,
        in_specs=[pl.BlockSpec(memory_space=pltpu.VMEM)] * len(operands),
        out_specs=jax.tree.map(lambda _: pl.BlockSpec(memory_space=pltpu.VMEM), out_shape),
        compiler_params=pltpu.CompilerParams(vmem_limit_bytes=LIMIT),
    )(*operands)


def times_transposed(left, right):
    return lax.dot_general(left, right, (((1,), (1,)), ((), ())), preferred_element_type=F32)


def arrived(ref):
    total = ref[0].astype(F32)
    for sender in range(1, ref.shape[0]):
        total = total + ref[sender].astype(F32)
    return total


def repeat(ref, block):
    for receiver in range(ref.shape[0]):
        ref[receiver] = block


def shares_sum(shares, block):
    return jnp.sum(shares * block, axis=0, keepdims=True)


def whole(block):
    return jnp.sum(jnp.sum(block, axis=1, keepdims=True), axis=0, keepdims=True)


def round_kernel(weights, far, rounded):
    del far
    rounded[...] = weights[...].astype(BF16)


def keep_kernel(weights, rows, index, mine, count):
    depth, _, own = mine.shape
    core = lax.axis_index("c")
    place = core * depth + lax.axis_index("z")
    rounded = weights[...].astype(BF16)
    for level in range(depth):
        mine[level] = times_transposed(rounded, rows[core * depth + level])
    offset = index[...] - (lax.axis_index("row") * (CORES * depth * own) + place * own)
    low, high = offset & (LANES - 1), offset >> 7
    low_place = lax.broadcasted_iota(jnp.int32, (LANES, LANES), 0)
    high_place = lax.broadcasted_iota(jnp.int32, (SUBLANES, LANES), 0)
    drawn = jnp.zeros((SUBLANES, LANES), F32)
    for line in range(index.shape[0]):
        is_low = (low[line : line + 1] == low_place).astype(F32).astype(BF16)
        is_high = (high[line : line + 1] == high_place).astype(F32).astype(BF16)
        drawn = drawn + times_transposed(is_high, is_low)
    for part in range(own // LANES):
        count[:, part * LANES : (part + 1) * LANES] = drawn[part : part + 1]


def code_kernel(mine, parcel, sent):
    depth, classes, own = mine.shape
    rounded = parcel[depth * own :]
    for level in range(depth):
        value = mine[level] + times_transposed(rounded, parcel[level * own : (level + 1) * own])
        value = value - value[-1:]
        largest = jnp.max(jnp.abs(value), axis=0, keepdims=True)
        scale = jnp.minimum(jnp.floor(largest * (TOP / REACH)) + 1.0, TOP)
        code = jnp.floor(value * (TOP * TOP / REACH / scale) + 0.5)
        code = jnp.clip(code, -TOP, TOP)
        last = lax.broadcasted_iota(jnp.int32, value.shape, 0) == classes - 1
        sent[level] = jnp.where(last, scale, code).astype(jnp.int32).astype(jnp.int16)


def misfit_kernel(came, labels, shares, sent):
    depth, classes, own = came.shape
    logits = jnp.zeros((classes, own), F32)
    for sender in range(depth):
        code = came[sender].astype(jnp.int32).astype(F32)
        logits = logits + code * (code[-1:] * (REACH / TOP / TOP))
    kind = lax.broadcasted_iota(jnp.int32, logits.shape, 0)
    logits = jnp.where(kind == classes - 1, 0.0, logits)
    exponent = jnp.exp(logits - jnp.max(logits, axis=0, keepdims=True))
    share = exponent / jnp.sum(exponent, axis=0, keepdims=True)
    shares[...] = share
    lines = own // LANES
    first = (lax.axis_index("c") * depth + lax.axis_index("z")) * lines
    label = jnp.concatenate([labels[pl.ds(first + line, 1), :] for line in range(lines)], axis=1)
    repeat(sent, (share - (label == kind).astype(F32)).astype(BF16))


def columns(came, rows, parcel):
    core = lax.axis_index("c")
    depth, _, own = came.shape
    near = jnp.dot(came[0], rows[core * depth], preferred_element_type=F32)
    far = jnp.dot(came[0], parcel[:own], preferred_element_type=F32)
    for level in range(1, depth):
        near = near + jnp.dot(came[level], rows[core * depth + level], preferred_element_type=F32)
        far = far + jnp.dot(came[level], parcel[level * own : (level + 1) * own], preferred_element_type=F32)
    return near, far


def misfit_columns_kernel(came, rows, parcel, weights, part):
    own, far = columns(came, rows, parcel)
    width = own.shape[1]
    part[0, :, :width] = own
    part[0, :, width:] = far
    part[1, :, :width] = weights[...]
    part[1, :, width:] = jnp.zeros_like(far)


def image_columns_kernel(came, rows, parcel, part):
    own, far = columns(came, rows, parcel)
    width = own.shape[1]
    part[:, :width] = own
    part[:, width:] = far


def add_cores(mine, far):
    width = mine.shape[1] // CORES
    return mine + jnp.concatenate([far[:, width:], far[:, :width]], axis=1)


def column_scale(code):
    return jnp.exp2(code * (1.0 / STEPS))


def gradient_pair_kernel(parts, weights, sent):
    core = lax.axis_index("c")
    both = add_cores(parts[core, 0], parts[1 - core, 0])
    weights[...] = add_cores(parts[core, 1], parts[1 - core, 1])
    largest = jnp.maximum(jnp.max(jnp.abs(both), axis=0, keepdims=True), SMALLEST)
    scale = jnp.floor(jnp.log2(largest) * STEPS) + 2.0
    code = jnp.clip(jnp.floor(both * (TOP / column_scale(scale)) + 0.5), -TOP, TOP)
    last = lax.broadcasted_iota(jnp.int32, both.shape, 0) == both.shape[0] - 1
    repeat(sent, jnp.where(last, scale, code).astype(jnp.int32).astype(jnp.int16))


def image_pair_kernel(parts, sent):
    core = lax.axis_index("c")
    repeat(sent, add_cores(parts[core], parts[1 - core]).astype(sent.dtype))


def respond(vector, rows, parcel, depth):
    core = lax.axis_index("c")
    _, users, width = rows.shape
    own, far = vector[:, :width].astype(BF16), vector[:, width:].astype(BF16)
    for level in range(depth):
        near = times_transposed(own, rows[core * depth + level])
        yield near + times_transposed(far, parcel[level * users : (level + 1) * users])


def gradient_kernel(users, came, weights, rows, parcel, residual, sent):
    value = jnp.zeros(weights.shape, F32)
    for sender in range(came.shape[0]):
        code = came[sender].astype(jnp.int32).astype(F32)
        value = value + code * (column_scale(code[-1:]) * (1.0 / TOP))
    last = lax.broadcasted_iota(jnp.int32, value.shape, 0) == value.shape[0] - 1
    value = jnp.where(last, 0.0, value)
    value = jnp.where(last, -jnp.sum(value, axis=0, keepdims=True), value)
    value = -(value / users + RIDGE_WEIGHT * weights[...])
    residual[...] = value
    for level, answer in enumerate(respond(value, rows, parcel, sent.shape[0])):
        sent[level] = answer.astype(BF16)


def weigh_kernel(came, shares, count, response, sent):
    value = arrived(came)
    response[...] = value
    share = shares[...]
    repeat(sent, (count[...] * (share * (value - shares_sum(share, value)))).astype(BF16))


def image_kernel(sub_total, came, residual, rows, parcel, image, sent):
    start = residual[...]
    value = arrived(came) / sub_total + RIDGE_WEIGHT * start
    image[...] = value
    _, classes, own = sent.shape
    lane = lax.broadcasted_iota(jnp.int32, (1, own), 1)
    line = jnp.zeros(lane.shape, F32)
    for which, product in enumerate((start * start, start * value, value * value)):
        left = whole(product)
        for piece in range(PIECES):
            head = left.astype(BF16).astype(F32)
            line = jnp.where(lane == which * PIECES + piece, head, line)
            left = left - head
    last = lax.broadcasted_iota(jnp.int32, (classes, own), 0) == classes - 1
    for level, answer in enumerate(respond(value, rows, parcel, sent.shape[0])):
        sent[level] = jnp.where(last, line, answer - answer[-1:]).astype(BF16)


def direction_kernel(came, response, shares, count, residual, image, base, direction, sent):
    got = arrived(came)
    classes, own = got.shape
    width = base.shape[1]
    line = got[-1:]
    lane = lax.broadcasted_iota(jnp.int32, line.shape, 1)

    def scalar(which):
        pieces = jnp.logical_and(lane >= which * PIECES, lane < (which + 1) * PIECES)
        return jnp.sum(jnp.where(pieces, line, 0.0), axis=1, keepdims=True)

    norm, curve, image_norm = scalar(0), scalar(1), scalar(2)
    step = norm / curve
    beta = jnp.maximum(image_norm / curve * step - 1.0, 0.0)
    start = residual[...]
    after = start - step * image[...]
    second = after + beta * start
    base[...] = step * start[:, :width]
    direction[...] = second[:, :width]
    image_response = jnp.where(lax.broadcasted_iota(jnp.int32, got.shape, 0) == classes - 1, 0.0, got)
    share = shares[...]
    value = (1.0 + beta) * response[...] - step * image_response
    centred = value - shares_sum(share, value)
    lane = lax.broadcasted_iota(jnp.int32, (1, LANES), 1)
    line = jnp.where(lane == 0, whole(after * after), whole(second * second))
    line = jnp.where(lane < 2, line, whole(count[...] * (share * (centred * centred))))
    repeat(sent, line)


def relay_kernel(came, sent):
    repeat(sent, arrived(came))


def step_kernel(sub_total, copies, came, residual, base, direction, gradient, newton_step):
    gradient[...] = -residual[:, : gradient.shape[1]]
    line = arrived(came)
    norm, square, spread = line[:, 0:1] / copies, line[:, 1:2] / copies, line[:, 2:3]
    curve = spread / sub_total + RIDGE_WEIGHT * square
    newton_step[...] = base[...] + norm / curve * direction[...]


def swap(block, axis):
    return lax.all_to_all(block, axis, 0, 0, tiled=True)


def array(*shape, dtype=F32):
    return jax.ShapeDtypeStruct(shape, dtype)


def body(covariates, labels, weights, sample_index):
    user_rows, width = covariates.shape
    classes = weights.shape[0]
    row_count, depth = lax.axis_size("row"), lax.axis_size("z")
    users = user_rows * row_count
    sub_total = sample_index.shape[0] * row_count
    own = user_rows // CORES // depth
    wide = CORES * width
    blocks = (depth, classes, own)
    rows = covariates.reshape(CORES * depth, own, width)
    labels = labels.reshape(-1, LANES)
    sample_index = sample_index.reshape(-1, LANES)

    half = user_rows // CORES
    far = lax.dynamic_slice_in_dim(covariates, (1 - lax.axis_index("c")) * half, half, 0)
    rounded = pl.pallas_call(
        round_kernel,
        out_shape=array(classes, width, dtype=BF16),
        in_specs=[pl.BlockSpec(memory_space=pltpu.VMEM), pl.BlockSpec(memory_space=pl.ANY)],
        out_specs=pl.BlockSpec(memory_space=pltpu.VMEM),
        compiler_params=pltpu.CompilerParams(vmem_limit_bytes=LIMIT),
    )(weights, far)
    parcel = jnp.concatenate([far, rounded], axis=0)
    parcel = lax.ppermute(parcel, "c", [(0, 1), (1, 0)])
    mine, count = kernel_call(keep_kernel, (array(*blocks), array(1, own)), weights, rows, sample_index)
    sent = kernel_call(code_kernel, array(*blocks, dtype=jnp.int16), mine, parcel)
    shares, sent = kernel_call(
        misfit_kernel, (array(classes, own), array(*blocks, dtype=BF16)), swap(sent, "z"), labels
    )

    part = kernel_call(
        misfit_columns_kernel, array(CORES, classes, wide), swap(sent, "z"), rows, parcel, weights
    )
    wide_weights, sent = kernel_call(
        gradient_pair_kernel,
        (array(classes, wide), array(row_count, classes, wide, dtype=jnp.int16)),
        lax.all_gather(part, "c", axis=0),
    )
    residual, sent = kernel_call(
        functools.partial(gradient_kernel, users),
        (array(classes, wide), array(*blocks, dtype=BF16)),
        swap(sent, "row"), wide_weights, rows, parcel,
    )
    response, sent = kernel_call(
        weigh_kernel, (array(classes, own), array(*blocks, dtype=BF16)), swap(sent, "z"), shares, count
    )
    part = kernel_call(image_columns_kernel, array(classes, wide), swap(sent, "z"), rows, parcel)
    sent = kernel_call(
        image_pair_kernel, array(row_count, classes, wide, dtype=BF16), lax.all_gather(part, "c", axis=0)
    )
    image, sent = kernel_call(
        functools.partial(image_kernel, sub_total),
        (array(classes, wide), array(*blocks, dtype=BF16)),
        swap(sent, "row"), residual, rows, parcel,
    )
    base, direction, sent = kernel_call(
        direction_kernel,
        (array(classes, width), array(classes, width), array(depth * CORES, 1, LANES)),
        swap(sent, "z"), response, shares, count, residual, image,
    )
    sent = kernel_call(relay_kernel, array(row_count, 1, LANES), swap(sent, ("z", "c")))
    return kernel_call(
        functools.partial(step_kernel, sub_total, row_count * CORES),
        (array(classes, width), array(classes, width)),
        swap(sent, "row"), residual, base, direction,
    )


def solution(mesh):
    rows, cols = mesh.devices.shape
    fine = Mesh(mesh.devices.reshape(rows, cols // CORES, CORES), ("row", "z", "c"))
    in_specs = (P("row", ("z", "c")), P("row"), P(None, ("z", "c")), P("row"))
    out_specs = (P(None, ("z", "c")), P(None, ("z", "c")))
    return jax.shard_map(body, mesh=fine, in_specs=in_specs, out_specs=out_specs, check_vma=False)
```

```python
import functools

import jax
import jax.numpy as jnp
from jax import lax
from jax.experimental import pallas as pl
from jax.experimental.pallas import tpu as pltpu
from jax.sharding import Mesh, PartitionSpec as P

RIDGE_WEIGHT = 0.004
F32, BF16 = jnp.float32, jnp.bfloat16
LANES, SUBLANES = 128, 8
PIECES = 3
CORES = 2
LIMIT = 24 * 1024 * 1024
TOP, REACH = 32767.0, 768.0
STEPS, SMALLEST = 128.0, 1e-30


def kernel_call(body, out_shape, *operands):
    return pl.pallas_call(
        body,
        out_shape=out_shape,
        in_specs=[pl.BlockSpec(memory_space=pltpu.VMEM)] * len(operands),
        out_specs=jax.tree.map(lambda _: pl.BlockSpec(memory_space=pltpu.VMEM), out_shape),
        compiler_params=pltpu.CompilerParams(vmem_limit_bytes=LIMIT),
    )(*operands)


def times_transposed(left, right):
    return lax.dot_general(left, right, (((1,), (1,)), ((), ())), preferred_element_type=F32)


def arrived(ref):
    total = ref[0].astype(F32)
    for sender in range(1, ref.shape[0]):
        total = total + ref[sender].astype(F32)
    return total


def repeat(ref, block):
    for receiver in range(ref.shape[0]):
        ref[receiver] = block


def shares_sum(shares, block):
    return jnp.sum(shares * block, axis=0, keepdims=True)


def whole(block):
    return jnp.sum(jnp.sum(block, axis=1, keepdims=True), axis=0, keepdims=True)


def round_kernel(weights, far, rounded):
    del far
    rounded[...] = weights[...].astype(BF16)


def keep_kernel(weights, rows, index, mine, count):
    depth, _, own = mine.shape
    core = lax.axis_index("c")
    place = core * depth + lax.axis_index("z")
    rounded = weights[...].astype(BF16)
    for level in range(depth):
        mine[level] = times_transposed(rounded, rows[core * depth + level])
    offset = index[...] - (lax.axis_index("row") * (CORES * depth * own) + place * own)
    low, high = offset & (LANES - 1), offset >> 7
    low_place = lax.broadcasted_iota(jnp.int32, (LANES, LANES), 0)
    high_place = lax.broadcasted_iota(jnp.int32, (SUBLANES, LANES), 0)
    drawn = jnp.zeros((SUBLANES, LANES), F32)
    for line in range(index.shape[0]):
        is_low = (low[line : line + 1] == low_place).astype(F32).astype(BF16)
        is_high = (high[line : line + 1] == high_place).astype(F32).astype(BF16)
        drawn = drawn + times_transposed(is_high, is_low)
    for part in range(own // LANES):
        count[:, part * LANES : (part + 1) * LANES] = drawn[part : part + 1]


def code_kernel(mine, parcel, sent):
    depth, classes, own = mine.shape
    rounded = parcel[depth * own :]
    for level in range(depth):
        value = mine[level] + times_transposed(rounded, parcel[level * own : (level + 1) * own])
        value = value - value[-1:]
        largest = jnp.max(jnp.abs(value), axis=0, keepdims=True)
        scale = jnp.minimum(jnp.floor(largest * (TOP / REACH)) + 1.0, TOP)
        code = jnp.floor(value * (TOP * TOP / REACH / scale) + 0.5)
        code = jnp.clip(code, -TOP, TOP)
        last = lax.broadcasted_iota(jnp.int32, value.shape, 0) == classes - 1
        sent[level] = jnp.where(last, scale, code).astype(jnp.int32).astype(jnp.int16)


def misfit_kernel(came, labels, shares, sent):
    depth, classes, own = came.shape
    logits = jnp.zeros((classes, own), F32)
    for sender in range(depth):
        code = came[sender].astype(jnp.int32).astype(F32)
        logits = logits + code * (code[-1:] * (REACH / TOP / TOP))
    kind = lax.broadcasted_iota(jnp.int32, logits.shape, 0)
    logits = jnp.where(kind == classes - 1, 0.0, logits)
    exponent = jnp.exp(logits - jnp.max(logits, axis=0, keepdims=True))
    share = exponent / jnp.sum(exponent, axis=0, keepdims=True)
    shares[...] = share
    lines = own // LANES
    first = (lax.axis_index("c") * depth + lax.axis_index("z")) * lines
    label = jnp.concatenate([labels[pl.ds(first + line, 1), :] for line in range(lines)], axis=1)
    repeat(sent, (share - (label == kind).astype(F32)).astype(BF16))


def columns(came, rows, parcel):
    core = lax.axis_index("c")
    depth, _, own = came.shape
    near = jnp.dot(came[0], rows[core * depth], preferred_element_type=F32)
    far = jnp.dot(came[0], parcel[:own], preferred_element_type=F32)
    for level in range(1, depth):
        near = near + jnp.dot(came[level], rows[core * depth + level], preferred_element_type=F32)
        far = far + jnp.dot(came[level], parcel[level * own : (level + 1) * own], preferred_element_type=F32)
    return near, far


def misfit_columns_kernel(came, rows, parcel, weights, part):
    own, far = columns(came, rows, parcel)
    width = own.shape[1]
    part[0, :, :width] = own
    part[0, :, width:] = far
    part[1, :, :width] = weights[...]
    part[1, :, width:] = jnp.zeros_like(far)


def image_columns_kernel(came, rows, parcel, part):
    own, far = columns(came, rows, parcel)
    width = own.shape[1]
    part[:, :width] = own
    part[:, width:] = far


def add_cores(mine, far):
    width = mine.shape[1] // CORES
    return mine + jnp.concatenate([far[:, width:], far[:, :width]], axis=1)


def scale_of(code):
    return jnp.exp2(code * (1.0 / STEPS))


def halves(shape):
    width = shape[1] // CORES
    column = lax.broadcasted_iota(jnp.int32, shape, 1)
    last = lax.broadcasted_iota(jnp.int32, shape, 0) == shape[0] - 1
    start = jnp.logical_or(column == 0, column == width)
    return jnp.logical_and(last, start), lax.broadcasted_iota(jnp.int32, (1, shape[1]), 1) < width


def gradient_pair_kernel(parts, weights, sent):
    core = lax.axis_index("c")
    both = add_cores(parts[core, 0], parts[1 - core, 0])
    weights[...] = add_cores(parts[core, 1], parts[1 - core, 1])
    spot, first = halves(both.shape)
    size = jnp.max(jnp.abs(both), axis=0, keepdims=True)
    left = jnp.max(jnp.where(first, size, SMALLEST), axis=1, keepdims=True)
    right = jnp.max(jnp.where(first, SMALLEST, size), axis=1, keepdims=True)
    scale = jnp.floor(jnp.log2(jnp.maximum(jnp.where(first, left, right), SMALLEST)) * STEPS) + 2.0
    code = jnp.clip(jnp.floor(both * (TOP / scale_of(scale)) + 0.5), -TOP, TOP)
    repeat(sent, jnp.where(spot, scale, code).astype(jnp.int32).astype(jnp.int16))


def image_pair_kernel(parts, sent):
    core = lax.axis_index("c")
    repeat(sent, add_cores(parts[core], parts[1 - core]).astype(sent.dtype))


def respond(vector, rows, parcel, depth):
    core = lax.axis_index("c")
    _, users, width = rows.shape
    own, far = vector[:, :width].astype(BF16), vector[:, width:].astype(BF16)
    for level in range(depth):
        near = times_transposed(own, rows[core * depth + level])
        yield near + times_transposed(far, parcel[level * users : (level + 1) * users])


def gradient_kernel(users, came, weights, rows, parcel, residual, sent):
    value = jnp.zeros(weights.shape, F32)
    spot, first = halves(value.shape)
    width = value.shape[1] // CORES
    for sender in range(came.shape[0]):
        code = came[sender].astype(jnp.int32).astype(F32)
        scale = jnp.where(first, code[-1:, :1], code[-1:, width : width + 1])
        value = value + code * (scale_of(scale) * (1.0 / TOP))
    value = jnp.where(spot, 0.0, value)
    value = jnp.where(spot, -jnp.sum(value, axis=0, keepdims=True), value)
    value = -(value / users + RIDGE_WEIGHT * weights[...])
    residual[...] = value
    for level, answer in enumerate(respond(value, rows, parcel, sent.shape[0])):
        sent[level] = answer.astype(BF16)


def weigh_kernel(came, shares, count, response, sent):
    value = arrived(came)
    response[...] = value
    share = shares[...]
    repeat(sent, (count[...] * (share * (value - shares_sum(share, value)))).astype(BF16))


def image_kernel(sub_total, came, residual, rows, parcel, image, sent):
    start = residual[...]
    value = arrived(came) / sub_total + RIDGE_WEIGHT * start
    image[...] = value
    _, classes, own = sent.shape
    lane = lax.broadcasted_iota(jnp.int32, (1, own), 1)
    line = jnp.zeros(lane.shape, F32)
    for which, product in enumerate((start * start, start * value, value * value)):
        left = whole(product)
        for piece in range(PIECES):
            head = left.astype(BF16).astype(F32)
            line = jnp.where(lane == which * PIECES + piece, head, line)
            left = left - head
    last = lax.broadcasted_iota(jnp.int32, (classes, own), 0) == classes - 1
    for level, answer in enumerate(respond(value, rows, parcel, sent.shape[0])):
        sent[level] = jnp.where(last, line, answer - answer[-1:]).astype(BF16)


def direction_kernel(came, response, shares, count, residual, image, base, direction, sent):
    got = arrived(came)
    classes, own = got.shape
    width = base.shape[1]
    line = got[-1:]
    lane = lax.broadcasted_iota(jnp.int32, line.shape, 1)

    def scalar(which):
        pieces = jnp.logical_and(lane >= which * PIECES, lane < (which + 1) * PIECES)
        return jnp.sum(jnp.where(pieces, line, 0.0), axis=1, keepdims=True)

    norm, curve, image_norm = scalar(0), scalar(1), scalar(2)
    step = norm / curve
    beta = jnp.maximum(image_norm / curve * step - 1.0, 0.0)
    start = residual[...]
    after = start - step * image[...]
    second = after + beta * start
    base[...] = step * start[:, :width]
    direction[...] = second[:, :width]
    image_response = jnp.where(lax.broadcasted_iota(jnp.int32, got.shape, 0) == classes - 1, 0.0, got)
    share = shares[...]
    value = (1.0 + beta) * response[...] - step * image_response
    centred = value - shares_sum(share, value)
    lane = lax.broadcasted_iota(jnp.int32, (1, LANES), 1)
    line = jnp.where(lane == 0, whole(after * after), whole(second * second))
    line = jnp.where(lane < 2, line, whole(count[...] * (share * (centred * centred))))
    repeat(sent, line)


def relay_kernel(came, sent):
    repeat(sent, arrived(came))


def step_kernel(sub_total, copies, came, residual, base, direction, gradient, newton_step):
    gradient[...] = -residual[:, : gradient.shape[1]]
    line = arrived(came)
    norm, square, spread = line[:, 0:1] / copies, line[:, 1:2] / copies, line[:, 2:3]
    curve = spread / sub_total + RIDGE_WEIGHT * square
    newton_step[...] = base[...] + norm / curve * direction[...]


def swap(block, axis):
    return lax.all_to_all(block, axis, 0, 0, tiled=True)


def array(*shape, dtype=F32):
    return jax.ShapeDtypeStruct(shape, dtype)


def body(covariates, labels, weights, sample_index):
    user_rows, width = covariates.shape
    classes = weights.shape[0]
    row_count, depth = lax.axis_size("row"), lax.axis_size("z")
    users = user_rows * row_count
    sub_total = sample_index.shape[0] * row_count
    own = user_rows // CORES // depth
    wide = CORES * width
    blocks = (depth, classes, own)
    rows = covariates.reshape(CORES * depth, own, width)
    labels = labels.reshape(-1, LANES)
    sample_index = sample_index.reshape(-1, LANES)

    half = user_rows // CORES
    far = lax.dynamic_slice_in_dim(covariates, (1 - lax.axis_index("c")) * half, half, 0)
    rounded = pl.pallas_call(
        round_kernel,
        out_shape=array(classes, width, dtype=BF16),
        in_specs=[pl.BlockSpec(memory_space=pltpu.VMEM), pl.BlockSpec(memory_space=pl.ANY)],
        out_specs=pl.BlockSpec(memory_space=pltpu.VMEM),
        compiler_params=pltpu.CompilerParams(vmem_limit_bytes=LIMIT),
    )(weights, far)
    parcel = jnp.concatenate([far, rounded], axis=0)
    parcel = lax.ppermute(parcel, "c", [(0, 1), (1, 0)])
    mine, count = kernel_call(keep_kernel, (array(*blocks), array(1, own)), weights, rows, sample_index)
    sent = kernel_call(code_kernel, array(*blocks, dtype=jnp.int16), mine, parcel)
    shares, sent = kernel_call(
        misfit_kernel, (array(classes, own), array(*blocks, dtype=BF16)), swap(sent, "z"), labels
    )

    part = kernel_call(
        misfit_columns_kernel, array(CORES, classes, wide), swap(sent, "z"), rows, parcel, weights
    )
    wide_weights, sent = kernel_call(
        gradient_pair_kernel,
        (array(classes, wide), array(row_count, classes, wide, dtype=jnp.int16)),
        lax.all_gather(part, "c", axis=0),
    )
    residual, sent = kernel_call(
        functools.partial(gradient_kernel, users),
        (array(classes, wide), array(*blocks, dtype=BF16)),
        swap(sent, "row"), wide_weights, rows, parcel,
    )
    response, sent = kernel_call(
        weigh_kernel, (array(classes, own), array(*blocks, dtype=BF16)), swap(sent, "z"), shares, count
    )
    part = kernel_call(image_columns_kernel, array(classes, wide), swap(sent, "z"), rows, parcel)
    sent = kernel_call(
        image_pair_kernel, array(row_count, classes, wide, dtype=BF16), lax.all_gather(part, "c", axis=0)
    )
    image, sent = kernel_call(
        functools.partial(image_kernel, sub_total),
        (array(classes, wide), array(*blocks, dtype=BF16)),
        swap(sent, "row"), residual, rows, parcel,
    )
    base, direction, sent = kernel_call(
        direction_kernel,
        (array(classes, width), array(classes, width), array(depth * CORES, 1, LANES)),
        swap(sent, "z"), response, shares, count, residual, image,
    )
    sent = kernel_call(relay_kernel, array(row_count, 1, LANES), swap(sent, ("z", "c")))
    return kernel_call(
        functools.partial(step_kernel, sub_total, row_count * CORES),
        (array(classes, width), array(classes, width)),
        swap(sent, "row"), residual, base, direction,
    )


def solution(mesh):
    rows, cols = mesh.devices.shape
    fine = Mesh(mesh.devices.reshape(rows, cols // CORES, CORES), ("row", "z", "c"))
    in_specs = (P("row", ("z", "c")), P("row"), P(None, ("z", "c")), P("row"))
    out_specs = (P(None, ("z", "c")), P(None, ("z", "c")))
    return jax.shard_map(body, mesh=fine, in_specs=in_specs, out_specs=out_specs, check_vma=False)
```

```python
import functools

import jax
import jax.numpy as jnp
from jax import lax
from jax.experimental import pallas as pl
from jax.experimental.pallas import tpu as pltpu
from jax.sharding import Mesh, PartitionSpec as P

RIDGE_WEIGHT = 0.004
F32, BF16 = jnp.float32, jnp.bfloat16
LANES, SUBLANES = 128, 8
PIECES = 3
CORES = 2
LIMIT = 24 * 1024 * 1024
TOP, REACH = 32767.0, 768.0
STEPS, SMALLEST = 128.0, 1e-30


def kernel_call(body, out_shape, *operands):
    return pl.pallas_call(
        body,
        out_shape=out_shape,
        in_specs=[pl.BlockSpec(memory_space=pltpu.VMEM)] * len(operands),
        out_specs=jax.tree.map(lambda _: pl.BlockSpec(memory_space=pltpu.VMEM), out_shape),
        compiler_params=pltpu.CompilerParams(vmem_limit_bytes=LIMIT),
    )(*operands)


def times_transposed(left, right):
    return lax.dot_general(left, right, (((1,), (1,)), ((), ())), preferred_element_type=F32)


def arrived(ref):
    total = ref[0].astype(F32)
    for sender in range(1, ref.shape[0]):
        total = total + ref[sender].astype(F32)
    return total


def repeat(ref, block):
    for receiver in range(ref.shape[0]):
        ref[receiver] = block


def shares_sum(shares, block):
    return jnp.sum(shares * block, axis=0, keepdims=True)


def whole(block):
    return jnp.sum(jnp.sum(block, axis=1, keepdims=True), axis=0, keepdims=True)


def round_kernel(weights, far, rounded):
    del far
    rounded[...] = weights[...].astype(BF16)


def keep_kernel(weights, rows, index, mine, count):
    depth, _, own = mine.shape
    core = lax.axis_index("c")
    place = core * depth + lax.axis_index("z")
    rounded = weights[...].astype(BF16)
    for level in range(depth):
        mine[level] = times_transposed(rounded, rows[core * depth + level])
    offset = index[...] - (lax.axis_index("row") * (CORES * depth * own) + place * own)
    low, high = offset & (LANES - 1), offset >> 7
    low_place = lax.broadcasted_iota(jnp.int32, (LANES, LANES), 0)
    high_place = lax.broadcasted_iota(jnp.int32, (SUBLANES, LANES), 0)
    drawn = jnp.zeros((SUBLANES, LANES), F32)
    for line in range(index.shape[0]):
        is_low = (low[line : line + 1] == low_place).astype(F32).astype(BF16)
        is_high = (high[line : line + 1] == high_place).astype(F32).astype(BF16)
        drawn = drawn + times_transposed(is_high, is_low)
    for part in range(own // LANES):
        count[:, part * LANES : (part + 1) * LANES] = drawn[part : part + 1]


def code_kernel(mine, parcel, sent):
    depth, classes, own = mine.shape
    rounded = parcel[depth * own :]
    for level in range(depth):
        value = mine[level] + times_transposed(rounded, parcel[level * own : (level + 1) * own])
        value = value - value[-1:]
        largest = jnp.max(jnp.abs(value), axis=0, keepdims=True)
        scale = jnp.minimum(jnp.floor(largest * (TOP / REACH)) + 1.0, TOP)
        code = jnp.floor(value * (TOP * TOP / REACH / scale) + 0.5)
        code = jnp.clip(code, -TOP, TOP)
        last = lax.broadcasted_iota(jnp.int32, value.shape, 0) == classes - 1
        sent[level] = jnp.where(last, scale, code).astype(jnp.int32).astype(jnp.int16)


def misfit_kernel(came, labels, shares, sent):
    depth, classes, own = came.shape
    logits = jnp.zeros((classes, own), F32)
    for sender in range(depth):
        code = came[sender].astype(jnp.int32).astype(F32)
        logits = logits + code * (code[-1:] * (REACH / TOP / TOP))
    kind = lax.broadcasted_iota(jnp.int32, logits.shape, 0)
    logits = jnp.where(kind == classes - 1, 0.0, logits)
    exponent = jnp.exp(logits - jnp.max(logits, axis=0, keepdims=True))
    share = exponent / jnp.sum(exponent, axis=0, keepdims=True)
    shares[...] = share
    lines = own // LANES
    first = (lax.axis_index("c") * depth + lax.axis_index("z")) * lines
    label = jnp.concatenate([labels[pl.ds(first + line, 1), :] for line in range(lines)], axis=1)
    repeat(sent, (share - (label == kind).astype(F32)).astype(BF16))


def columns(came, rows, parcel):
    core = lax.axis_index("c")
    depth, _, own = came.shape
    near = jnp.dot(came[0], rows[core * depth], preferred_element_type=F32)
    far = jnp.dot(came[0], parcel[:own], preferred_element_type=F32)
    for level in range(1, depth):
        near = near + jnp.dot(came[level], rows[core * depth + level], preferred_element_type=F32)
        far = far + jnp.dot(came[level], parcel[level * own : (level + 1) * own], preferred_element_type=F32)
    return near, far


def misfit_columns_kernel(came, rows, parcel, weights, part):
    own, far = columns(came, rows, parcel)
    width = own.shape[1]
    part[0, :, :width] = own
    part[0, :, width:] = far
    part[1, :, :width] = weights[...]
    part[1, :, width:] = jnp.zeros_like(far)


def image_columns_kernel(came, rows, parcel, part):
    own, far = columns(came, rows, parcel)
    width = own.shape[1]
    part[:, :width] = own
    part[:, width:] = far


def add_cores(mine, far):
    width = mine.shape[1] // CORES
    return mine + jnp.concatenate([far[:, width:], far[:, :width]], axis=1)


def scale_of(code):
    return jnp.exp2(code * (1.0 / STEPS))


def scale_spot(shape):
    row, column = (lax.broadcasted_iota(jnp.int32, shape, axis) for axis in range(2))
    return jnp.logical_and(row == shape[0] - 1, column == 0)


def gradient_pair_kernel(parts, weights, sent):
    core = lax.axis_index("c")
    both = add_cores(parts[core, 0], parts[1 - core, 0])
    weights[...] = add_cores(parts[core, 1], parts[1 - core, 1])
    largest = jnp.max(jnp.max(jnp.abs(both), axis=0, keepdims=True), axis=1, keepdims=True)
    scale = jnp.floor(jnp.log2(jnp.maximum(largest, SMALLEST)) * STEPS) + 2.0
    code = jnp.clip(jnp.floor(both * (TOP / scale_of(scale)) + 0.5), -TOP, TOP)
    repeat(sent, jnp.where(scale_spot(both.shape), scale, code).astype(jnp.int32).astype(jnp.int16))


def image_pair_kernel(parts, sent):
    core = lax.axis_index("c")
    repeat(sent, add_cores(parts[core], parts[1 - core]).astype(sent.dtype))


def respond(vector, rows, parcel, depth):
    core = lax.axis_index("c")
    _, users, width = rows.shape
    own, far = vector[:, :width].astype(BF16), vector[:, width:].astype(BF16)
    for level in range(depth):
        near = times_transposed(own, rows[core * depth + level])
        yield near + times_transposed(far, parcel[level * users : (level + 1) * users])


def gradient_kernel(users, came, weights, rows, parcel, residual, sent):
    value = jnp.zeros(weights.shape, F32)
    spot = scale_spot(value.shape)
    for sender in range(came.shape[0]):
        code = came[sender].astype(jnp.int32).astype(F32)
        value = value + code * (scale_of(code[-1:, :1]) * (1.0 / TOP))
    value = jnp.where(spot, 0.0, value)
    value = jnp.where(spot, -jnp.sum(value, axis=0, keepdims=True), value)
    value = -(value / users + RIDGE_WEIGHT * weights[...])
    residual[...] = value
    for level, answer in enumerate(respond(value, rows, parcel, sent.shape[0])):
        sent[level] = answer.astype(BF16)


def weigh_kernel(came, shares, count, response, sent):
    value = arrived(came)
    response[...] = value
    share = shares[...]
    repeat(sent, (count[...] * (share * (value - shares_sum(share, value)))).astype(BF16))


def image_kernel(sub_total, came, residual, rows, parcel, image, sent):
    start = residual[...]
    value = arrived(came) / sub_total + RIDGE_WEIGHT * start
    image[...] = value
    _, classes, own = sent.shape
    lane = lax.broadcasted_iota(jnp.int32, (1, own), 1)
    line = jnp.zeros(lane.shape, F32)
    for which, product in enumerate((start * start, start * value, value * value)):
        left = whole(product)
        for piece in range(PIECES):
            head = left.astype(BF16).astype(F32)
            line = jnp.where(lane == which * PIECES + piece, head, line)
            left = left - head
    last = lax.broadcasted_iota(jnp.int32, (classes, own), 0) == classes - 1
    for level, answer in enumerate(respond(value, rows, parcel, sent.shape[0])):
        sent[level] = jnp.where(last, line, answer - answer[-1:]).astype(BF16)


def direction_kernel(came, response, shares, count, residual, image, base, direction, sent):
    got = arrived(came)
    classes, own = got.shape
    width = base.shape[1]
    line = got[-1:]
    lane = lax.broadcasted_iota(jnp.int32, line.shape, 1)

    def scalar(which):
        pieces = jnp.logical_and(lane >= which * PIECES, lane < (which + 1) * PIECES)
        return jnp.sum(jnp.where(pieces, line, 0.0), axis=1, keepdims=True)

    norm, curve, image_norm = scalar(0), scalar(1), scalar(2)
    step = norm / curve
    beta = jnp.maximum(image_norm / curve * step - 1.0, 0.0)
    start = residual[...]
    after = start - step * image[...]
    second = after + beta * start
    base[...] = step * start[:, :width]
    direction[...] = second[:, :width]
    image_response = jnp.where(lax.broadcasted_iota(jnp.int32, got.shape, 0) == classes - 1, 0.0, got)
    share = shares[...]
    value = (1.0 + beta) * response[...] - step * image_response
    centred = value - shares_sum(share, value)
    lane = lax.broadcasted_iota(jnp.int32, (1, LANES), 1)
    line = jnp.where(lane == 0, whole(after * after), whole(second * second))
    line = jnp.where(lane < 2, line, whole(count[...] * (share * (centred * centred))))
    repeat(sent, line)


def relay_kernel(came, sent):
    repeat(sent, arrived(came))


def step_kernel(sub_total, copies, came, residual, base, direction, gradient, newton_step):
    gradient[...] = -residual[:, : gradient.shape[1]]
    line = arrived(came)
    norm, square, spread = line[:, 0:1] / copies, line[:, 1:2] / copies, line[:, 2:3]
    curve = spread / sub_total + RIDGE_WEIGHT * square
    newton_step[...] = base[...] + norm / curve * direction[...]


def swap(block, axis):
    return lax.all_to_all(block, axis, 0, 0, tiled=True)


def array(*shape, dtype=F32):
    return jax.ShapeDtypeStruct(shape, dtype)


def body(covariates, labels, weights, sample_index):
    user_rows, width = covariates.shape
    classes = weights.shape[0]
    row_count, depth = lax.axis_size("row"), lax.axis_size("z")
    users = user_rows * row_count
    sub_total = sample_index.shape[0] * row_count
    own = user_rows // CORES // depth
    wide = CORES * width
    blocks = (depth, classes, own)
    rows = covariates.reshape(CORES * depth, own, width)
    labels = labels.reshape(-1, LANES)
    sample_index = sample_index.reshape(-1, LANES)

    half = user_rows // CORES
    far = lax.dynamic_slice_in_dim(covariates, (1 - lax.axis_index("c")) * half, half, 0)
    rounded = pl.pallas_call(
        round_kernel,
        out_shape=array(classes, width, dtype=BF16),
        in_specs=[pl.BlockSpec(memory_space=pltpu.VMEM), pl.BlockSpec(memory_space=pl.ANY)],
        out_specs=pl.BlockSpec(memory_space=pltpu.VMEM),
        compiler_params=pltpu.CompilerParams(vmem_limit_bytes=LIMIT),
    )(weights, far)
    parcel = jnp.concatenate([far, rounded], axis=0)
    parcel = lax.ppermute(parcel, "c", [(0, 1), (1, 0)])
    mine, count = kernel_call(keep_kernel, (array(*blocks), array(1, own)), weights, rows, sample_index)
    sent = kernel_call(code_kernel, array(*blocks, dtype=jnp.int16), mine, parcel)
    shares, sent = kernel_call(
        misfit_kernel, (array(classes, own), array(*blocks, dtype=BF16)), swap(sent, "z"), labels
    )

    part = kernel_call(
        misfit_columns_kernel, array(CORES, classes, wide), swap(sent, "z"), rows, parcel, weights
    )
    wide_weights, sent = kernel_call(
        gradient_pair_kernel,
        (array(classes, wide), array(row_count, classes, wide, dtype=jnp.int16)),
        lax.all_gather(part, "c", axis=0),
    )
    residual, sent = kernel_call(
        functools.partial(gradient_kernel, users),
        (array(classes, wide), array(*blocks, dtype=BF16)),
        swap(sent, "row"), wide_weights, rows, parcel,
    )
    response, sent = kernel_call(
        weigh_kernel, (array(classes, own), array(*blocks, dtype=BF16)), swap(sent, "z"), shares, count
    )
    part = kernel_call(image_columns_kernel, array(classes, wide), swap(sent, "z"), rows, parcel)
    sent = kernel_call(
        image_pair_kernel, array(row_count, classes, wide, dtype=BF16), lax.all_gather(part, "c", axis=0)
    )
    image, sent = kernel_call(
        functools.partial(image_kernel, sub_total),
        (array(classes, wide), array(*blocks, dtype=BF16)),
        swap(sent, "row"), residual, rows, parcel,
    )
    base, direction, sent = kernel_call(
        direction_kernel,
        (array(classes, width), array(classes, width), array(row_count * CORES, 1, LANES)),
        swap(sent, "z"), response, shares, count, residual, image,
    )
    sent = kernel_call(relay_kernel, array(depth, 1, LANES), swap(sent, ("row", "c")))
    return kernel_call(
        functools.partial(step_kernel, sub_total, row_count * CORES),
        (array(classes, width), array(classes, width)),
        swap(sent, "z"), residual, base, direction,
    )


def solution(mesh):
    rows, cols = mesh.devices.shape
    fine = Mesh(mesh.devices.reshape(rows, cols // CORES, CORES), ("row", "z", "c"))
    in_specs = (P("row", ("z", "c")), P("row"), P(None, ("z", "c")), P("row"))
    out_specs = (P(None, ("z", "c")), P(None, ("z", "c")))
    return jax.shard_map(body, mesh=fine, in_specs=in_specs, out_specs=out_specs, check_vma=False)
```

```python
import functools

import jax
import jax.numpy as jnp
from jax import lax
from jax.experimental import pallas as pl
from jax.experimental.pallas import tpu as pltpu
from jax.sharding import Mesh, PartitionSpec as P

RIDGE_WEIGHT = 0.004
F32, BF16 = jnp.float32, jnp.bfloat16
LANES, SUBLANES = 128, 8
PIECES = 3
CORES = 2
LIMIT = 24 * 1024 * 1024
TOP, REACH = 32767.0, 768.0
STEPS, SMALLEST = 128.0, 1e-30


def kernel_call(body, out_shape, *operands):
    return pl.pallas_call(
        body,
        out_shape=out_shape,
        in_specs=[pl.BlockSpec(memory_space=pltpu.VMEM)] * len(operands),
        out_specs=jax.tree.map(lambda _: pl.BlockSpec(memory_space=pltpu.VMEM), out_shape),
        compiler_params=pltpu.CompilerParams(vmem_limit_bytes=LIMIT),
    )(*operands)


def times_transposed(left, right):
    return lax.dot_general(left, right, (((1,), (1,)), ((), ())), preferred_element_type=F32)


def arrived(ref):
    total = ref[0].astype(F32)
    for sender in range(1, ref.shape[0]):
        total = total + ref[sender].astype(F32)
    return total


def repeat(ref, block):
    for receiver in range(ref.shape[0]):
        ref[receiver] = block


def shares_sum(shares, block):
    return jnp.sum(shares * block, axis=0, keepdims=True)


def whole(block):
    return jnp.sum(jnp.sum(block, axis=1, keepdims=True), axis=0, keepdims=True)


def round_kernel(weights, far, rounded):
    del far
    rounded[...] = weights[...].astype(BF16)


def keep_kernel(weights, rows, index, mine, count):
    depth, _, own = mine.shape
    core = lax.axis_index("c")
    place = core * depth + lax.axis_index("z")
    rounded = weights[...].astype(BF16)
    for level in range(depth):
        mine[level] = times_transposed(rounded, rows[core * depth + level])
    offset = index[...] - (lax.axis_index("row") * (CORES * depth * own) + place * own)
    low, high = offset & (LANES - 1), offset >> 7
    low_place = lax.broadcasted_iota(jnp.int32, (LANES, LANES), 0)
    high_place = lax.broadcasted_iota(jnp.int32, (SUBLANES, LANES), 0)
    drawn = jnp.zeros((SUBLANES, LANES), F32)
    for line in range(index.shape[0]):
        is_low = (low[line : line + 1] == low_place).astype(F32).astype(BF16)
        is_high = (high[line : line + 1] == high_place).astype(F32).astype(BF16)
        drawn = drawn + times_transposed(is_high, is_low)
    for part in range(own // LANES):
        count[:, part * LANES : (part + 1) * LANES] = drawn[part : part + 1]


def code_kernel(mine, parcel, sent):
    depth, classes, own = mine.shape
    rounded = parcel[depth * own :]
    for level in range(depth):
        value = mine[level] + times_transposed(rounded, parcel[level * own : (level + 1) * own])
        value = value - value[-1:]
        largest = jnp.max(jnp.abs(value), axis=0, keepdims=True)
        scale = jnp.minimum(jnp.floor(largest * (TOP / REACH)) + 1.0, TOP)
        code = jnp.floor(value * (TOP * TOP / REACH / scale) + 0.5)
        code = jnp.clip(code, -TOP, TOP)
        last = lax.broadcasted_iota(jnp.int32, value.shape, 0) == classes - 1
        sent[level] = jnp.where(last, scale, code).astype(jnp.int32).astype(jnp.int16)


def misfit_kernel(came, labels, shares, sent):
    depth, classes, own = came.shape
    logits = jnp.zeros((classes, own), F32)
    for sender in range(depth):
        code = came[sender].astype(jnp.int32).astype(F32)
        logits = logits + code * (code[-1:] * (REACH / TOP / TOP))
    kind = lax.broadcasted_iota(jnp.int32, logits.shape, 0)
    logits = jnp.where(kind == classes - 1, 0.0, logits)
    exponent = jnp.exp(logits - jnp.max(logits, axis=0, keepdims=True))
    share = exponent / jnp.sum(exponent, axis=0, keepdims=True)
    shares[...] = share
    lines = own // LANES
    first = (lax.axis_index("c") * depth + lax.axis_index("z")) * lines
    label = jnp.concatenate([labels[pl.ds(first + line, 1), :] for line in range(lines)], axis=1)
    repeat(sent, (share - (label == kind).astype(F32)).astype(BF16))


def columns(came, rows, parcel):
    core = lax.axis_index("c")
    depth, _, own = came.shape
    near = jnp.dot(came[0], rows[core * depth], preferred_element_type=F32)
    far = jnp.dot(came[0], parcel[:own], preferred_element_type=F32)
    for level in range(1, depth):
        near = near + jnp.dot(came[level], rows[core * depth + level], preferred_element_type=F32)
        far = far + jnp.dot(came[level], parcel[level * own : (level + 1) * own], preferred_element_type=F32)
    return near, far


def misfit_columns_kernel(came, rows, parcel, weights, part):
    own, far = columns(came, rows, parcel)
    width = own.shape[1]
    part[0, :, :width] = own
    part[0, :, width:] = far
    part[1, :, :width] = weights[...]
    part[1, :, width:] = jnp.zeros_like(far)


def image_columns_kernel(came, rows, parcel, part):
    own, far = columns(came, rows, parcel)
    width = own.shape[1]
    part[:, :width] = own
    part[:, width:] = far


def add_cores(mine, far):
    width = mine.shape[1] // CORES
    return mine + jnp.concatenate([far[:, width:], far[:, :width]], axis=1)


def scale_of(code):
    return jnp.exp2(code * (1.0 / STEPS))


def scale_spot(shape):
    row, column = (lax.broadcasted_iota(jnp.int32, shape, axis) for axis in range(2))
    return jnp.logical_and(row == shape[0] - 1, column == 0)


def gradient_pair_kernel(parts, weights, sent):
    core = lax.axis_index("c")
    both = add_cores(parts[core, 0], parts[1 - core, 0])
    weights[...] = add_cores(parts[core, 1], parts[1 - core, 1])
    largest = jnp.max(jnp.max(jnp.abs(both), axis=0, keepdims=True), axis=1, keepdims=True)
    scale = jnp.floor(jnp.log2(jnp.maximum(largest, SMALLEST)) * STEPS) + 2.0
    code = jnp.clip(jnp.floor(both * (TOP / scale_of(scale)) + 0.5), -TOP, TOP)
    repeat(sent, jnp.where(scale_spot(both.shape), scale, code).astype(jnp.int32).astype(jnp.int16))


def image_pair_kernel(parts, sent):
    core = lax.axis_index("c")
    repeat(sent, add_cores(parts[core], parts[1 - core]).astype(sent.dtype))


def respond(vector, rows, parcel, depth):
    core = lax.axis_index("c")
    _, users, width = rows.shape
    own, far = vector[:, :width].astype(BF16), vector[:, width:].astype(BF16)
    for level in range(depth):
        near = times_transposed(own, rows[core * depth + level])
        yield near + times_transposed(far, parcel[level * users : (level + 1) * users])


def gradient_kernel(users, came, weights, rows, parcel, residual, sent):
    value = jnp.zeros(weights.shape, F32)
    spot = scale_spot(value.shape)
    for sender in range(came.shape[0]):
        code = came[sender].astype(jnp.int32).astype(F32)
        value = value + code * (scale_of(code[-1:, :1]) * (1.0 / TOP))
    value = jnp.where(spot, 0.0, value)
    value = jnp.where(spot, -jnp.sum(value, axis=0, keepdims=True), value)
    value = -(value / users + RIDGE_WEIGHT * weights[...])
    residual[...] = value
    for level, answer in enumerate(respond(value, rows, parcel, sent.shape[0])):
        sent[level] = answer.astype(BF16)


def weigh_kernel(came, shares, count, response, sent):
    value = arrived(came)
    response[...] = value
    share = shares[...]
    repeat(sent, (count[...] * (share * (value - shares_sum(share, value)))).astype(BF16))


def image_kernel(sub_total, came, residual, rows, parcel, image, sent):
    start = residual[...]
    value = arrived(came) / sub_total + RIDGE_WEIGHT * start
    image[...] = value
    _, classes, own = sent.shape
    lane = lax.broadcasted_iota(jnp.int32, (1, own), 1)
    line = jnp.zeros(lane.shape, F32)
    for which, product in enumerate((start * start, start * value, value * value)):
        left = whole(product)
        for piece in range(PIECES):
            head = left.astype(BF16).astype(F32)
            line = jnp.where(lane == which * PIECES + piece, head, line)
            left = left - head
    last = lax.broadcasted_iota(jnp.int32, (classes, own), 0) == classes - 1
    for level, answer in enumerate(respond(value, rows, parcel, sent.shape[0])):
        sent[level] = jnp.where(last, line, answer - answer[-1:]).astype(BF16)


def direction_kernel(came, response, shares, count, residual, image, base, direction, sent):
    got = arrived(came)
    classes, own = got.shape
    width = base.shape[1]
    line = got[-1:]
    lane = lax.broadcasted_iota(jnp.int32, line.shape, 1)

    def scalar(which):
        pieces = jnp.logical_and(lane >= which * PIECES, lane < (which + 1) * PIECES)
        return jnp.sum(jnp.where(pieces, line, 0.0), axis=1, keepdims=True)

    norm, curve, image_norm = scalar(0), scalar(1), scalar(2)
    step = norm / curve
    beta = jnp.maximum(image_norm / curve * step - 1.0, 0.0)
    start = residual[...]
    after = start - step * image[...]
    second = after + beta * start
    base[...] = step * start[:, :width]
    direction[...] = second[:, :width]
    image_response = jnp.where(lax.broadcasted_iota(jnp.int32, got.shape, 0) == classes - 1, 0.0, got)
    share = shares[...]
    value = (1.0 + beta) * response[...] - step * image_response
    centred = value - shares_sum(share, value)
    lane = lax.broadcasted_iota(jnp.int32, (1, LANES), 1)
    line = jnp.where(lane == 0, whole(after * after), whole(second * second))
    line = jnp.where(lane < 2, line, whole(count[...] * (share * (centred * centred))))
    repeat(sent, line)


def relay_kernel(came, sent):
    repeat(sent, arrived(came))


def step_kernel(sub_total, copies, came, residual, base, direction, gradient, newton_step):
    gradient[...] = -residual[:, : gradient.shape[1]]
    line = arrived(came)
    norm, square, spread = line[:, 0:1] / copies, line[:, 1:2] / copies, line[:, 2:3]
    curve = spread / sub_total + RIDGE_WEIGHT * square
    newton_step[...] = base[...] + norm / curve * direction[...]


def swap(block, axis):
    return lax.all_to_all(block, axis, 0, 0, tiled=True)


def array(*shape, dtype=F32):
    return jax.ShapeDtypeStruct(shape, dtype)


def body(covariates, labels, weights, sample_index):
    user_rows, width = covariates.shape
    classes = weights.shape[0]
    row_count, depth = lax.axis_size("row"), lax.axis_size("z")
    users = user_rows * row_count
    sub_total = sample_index.shape[0] * row_count
    own = user_rows // CORES // depth
    wide = CORES * width
    blocks = (depth, classes, own)
    rows = covariates.reshape(CORES * depth, own, width)
    labels = labels.reshape(-1, LANES)
    sample_index = sample_index.reshape(-1, LANES)

    half = user_rows // CORES
    far = lax.dynamic_slice_in_dim(covariates, (1 - lax.axis_index("c")) * half, half, 0)
    rounded = pl.pallas_call(
        round_kernel,
        out_shape=array(classes, width, dtype=BF16),
        in_specs=[pl.BlockSpec(memory_space=pltpu.VMEM), pl.BlockSpec(memory_space=pl.ANY)],
        out_specs=pl.BlockSpec(memory_space=pltpu.VMEM),
        compiler_params=pltpu.CompilerParams(vmem_limit_bytes=LIMIT),
    )(weights, far)
    parcel = jnp.concatenate([far, rounded], axis=0)
    parcel = lax.ppermute(parcel, "c", [(0, 1), (1, 0)])
    mine, count = kernel_call(keep_kernel, (array(*blocks), array(1, own)), weights, rows, sample_index)
    sent = kernel_call(code_kernel, array(*blocks, dtype=jnp.int16), mine, parcel)
    shares, sent = kernel_call(
        misfit_kernel, (array(classes, own), array(*blocks, dtype=BF16)), swap(sent, "z"), labels
    )

    part = kernel_call(
        misfit_columns_kernel, array(CORES, classes, wide), swap(sent, "z"), rows, parcel, weights
    )
    wide_weights, sent = kernel_call(
        gradient_pair_kernel,
        (array(classes, wide), array(row_count, classes, wide, dtype=jnp.int16)),
        lax.all_gather(part, "c", axis=0),
    )
    residual, sent = kernel_call(
        functools.partial(gradient_kernel, users),
        (array(classes, wide), array(*blocks, dtype=BF16)),
        swap(sent, "row"), wide_weights, rows, parcel,
    )
    response, sent = kernel_call(
        weigh_kernel, (array(classes, own), array(*blocks, dtype=BF16)), swap(sent, "z"), shares, count
    )
    part = kernel_call(image_columns_kernel, array(classes, wide), swap(sent, "z"), rows, parcel)
    sent = kernel_call(
        image_pair_kernel, array(row_count, classes, wide, dtype=BF16), lax.all_gather(part, "c", axis=0)
    )
    image, sent = kernel_call(
        functools.partial(image_kernel, sub_total),
        (array(classes, wide), array(*blocks, dtype=BF16)),
        swap(sent, "row"), residual, rows, parcel,
    )
    base, direction, sent = kernel_call(
        direction_kernel,
        (array(classes, width), array(classes, width), array(depth * CORES, 1, LANES)),
        swap(sent, "z"), response, shares, count, residual, image,
    )
    sent = kernel_call(relay_kernel, array(row_count, 1, LANES), swap(sent, ("z", "c")))
    return kernel_call(
        functools.partial(step_kernel, sub_total, row_count * CORES),
        (array(classes, width), array(classes, width)),
        swap(sent, "row"), residual, base, direction,
    )


def solution(mesh):
    rows, cols = mesh.devices.shape
    fine = Mesh(mesh.devices.reshape(rows, cols // CORES, CORES), ("row", "z", "c"))
    in_specs = (P("row", ("z", "c")), P("row"), P(None, ("z", "c")), P("row"))
    out_specs = (P(None, ("z", "c")), P(None, ("z", "c")))
    return jax.shard_map(body, mesh=fine, in_specs=in_specs, out_specs=out_specs, check_vma=False)
```
